256 devices in a mesh: row: 8 (over x_hi, y), col: 32 (over x_lo, z, core).
Axes of the slice: x: 4 (x_hi: 2, x_lo: 2; x = x_hi * 2 + x_lo), y: 4, z: 8, core: 2. Of those that a mesh axis runs over, the one named last changes fastest.
Arguments:
- features: bfloat16 [65536, 256], P(('col', 'row')), may hold values from -6 to 6
- edge_tiles: bfloat16 [8, 6144, 128, 128], P('row', 'col'), may hold values from 0 to 0.020874023
- tile_slot: int32 [8, 6144], P('row', 'col'), may hold values from 0 to 1023, as said below
- tile_count: int32 [8, 32], P('row', 'col'), may hold values from 24 to 192, as said below
- weight: bfloat16 [256, 256], replicated, may hold values from -0.375 to 0.375
- cotangent: bfloat16 [65536, 256], P(('row', 'col')), may hold values from -6 to 6
Outputs:
- layer_out: bfloat16 [65536, 256], P(('row', 'col'))
- weight_grad: float32 [256, 256], replicated
- feature_grad: bfloat16 [65536, 256], P(('col', 'row'))
The draws below stay inside these ranges and needn't reach their ends.
Inputs may be any that keep to these rules, and one draw needn't show every extreme that they name: `tile_slot`: the positions of the 192 slots of one device are distinct cells of its block's tile grid, numbered row by row. `tile_count`: some device has all 192 slots live.
All inputs are finite; a program needn't handle non-finite values.
Results may differ from the reference program's by a relative error of at most 0.0061.
Values may be sent and summed in bfloat16 or wider, within the bound.
A program may use at most 128 MiB of HBM per device.

```python
import math
import jax
import jax.numpy as jnp
from jax import lax

H = 256
TILE = 128
NODE_DEV = 256
TILE_DEV = 192
NODES = 65536
N_ROW = 8
N_COL = 32


def draw_tile_slot(key, part):
    grid_cells = NODE_DEV * N_COL // TILE * (NODE_DEV * N_ROW // TILE)
    device_keys = jax.random.split(key, N_ROW * N_COL)

    def shuffle(device_key):
        return jax.random.permutation(device_key, grid_cells)[:TILE_DEV]
    positions = jax.vmap(shuffle)(device_keys)
    return positions.reshape(N_ROW, N_COL * TILE_DEV).astype(jnp.int32)


def draw_tile_count(key, part):
    devices_all = N_ROW * N_COL
    key_one, key_two, key_three = jax.random.split(jax.random.fold_in(key, 7), 3)
    counts = jax.random.randint(key_one, (devices_all,), TILE_DEV // 8, TILE_DEV + 1)
    busiest = jax.random.randint(key_two, (), 0, devices_all)
    lightest = (busiest + 1 + jax.random.randint(key_three, (), 0, devices_all - 1)) % devices_all
    device_ids = jnp.arange(devices_all, dtype=jnp.int32)
    counts = jnp.where(device_ids == busiest, TILE_DEV, counts)
    counts = jnp.where(device_ids == lightest, TILE_DEV // 8, counts)
    return counts.reshape(N_ROW, N_COL).astype(jnp.int32)


def steps_of(rng, dims, cuts, least, top_value):
    def one(position, blocks):
        draws = jax.random.uniform(jax.random.fold_in(jax.random.fold_in(rng, 6), position), (blocks,), jnp.float32, least / len(cuts), top_value / len(cuts))
        return jnp.repeat(jnp.exp(draws), dims[position] // blocks).reshape((-1,) + (1,) * (len(dims) - position - 1))

    level = one(*cuts[0])
    for cut in cuts[1:]:
        level = level * one(*cut)
    return level


def noise(own_key, shape, spread, limit, cuts=(), kind=jnp.bfloat16):
    drawn = spread * jax.random.normal(own_key, shape, jnp.float32)
    if cuts:
        drawn = drawn * steps_of(own_key, shape, cuts, -0.22, 0.18)
    return jnp.clip(drawn, -limit, limit).astype(kind)


def setup_inputs(seed: int = 0) -> dict:
    arg_keys = jax.random.split(jax.random.key(seed), 7)
    features = noise(arg_keys[0], (NODES, H), 1.0, 6.0, ((0, 256),))
    edge_tiles = jnp.clip(0.020874023 * jax.random.uniform(arg_keys[1], (N_ROW, N_COL * TILE_DEV, TILE, TILE), jnp.float32) ** steps_of(arg_keys[1], (N_ROW, N_COL * TILE_DEV, TILE, TILE), ((0, 8), (1, 32)), -0.2, 0.2), 0.0, 0.020874023).astype(jnp.bfloat16)
    tile_slot = draw_tile_slot(jax.random.fold_in(arg_keys[6], 71), 0)
    tile_count = draw_tile_count(jax.random.fold_in(arg_keys[6], 71), 0)
    weight = noise(arg_keys[4], (H, H), H ** -0.5, 0.375)
    cotangent = noise(arg_keys[5], (NODES, H), 1.0, 6.0, ((0, 256),))
    return {"features": features, "edge_tiles": edge_tiles, "tile_slot": tile_slot, "tile_count": tile_count, "weight": weight, "cotangent": cotangent}


def reference(features, edge_tiles, tile_slot, tile_count, weight, cotangent):
    row_tiles = NODE_DEV * N_COL // TILE
    col_tiles = NODE_DEV * N_ROW // TILE
    total = N_ROW * N_COL * TILE_DEV
    slot_ids = jnp.arange(N_COL * TILE_DEV, dtype=jnp.int32)
    col_dev = slot_ids // TILE_DEV
    row_dev = jnp.arange(N_ROW, dtype=jnp.int32)[:, None]
    counts = tile_count[:, col_dev]
    live_mask = ((slot_ids % TILE_DEV)[None, :] < counts).reshape(total).astype(jnp.float32)
    grow = (row_dev * row_tiles + tile_slot // col_tiles).reshape(total).astype(jnp.int32)
    gcol = (col_dev[None, :] * col_tiles + tile_slot % col_tiles).reshape(total).astype(jnp.int32)
    block_size = math.gcd(512, total)
    blocks = total // block_size
    items = (edge_tiles.reshape(blocks, block_size, TILE, TILE),
             grow.reshape(blocks, block_size),
             gcol.reshape(blocks, block_size),
             live_mask.reshape(blocks, block_size))
    x_tiles_all = features.reshape(NODES // TILE, TILE, H)

    def forward_step(running, batch):
        tile_block, row_block, col_block, mask_block = batch
        x_tiles = x_tiles_all[col_block].astype(jnp.float32)
        product = jnp.einsum("gab,gbh->gah", tile_block.astype(jnp.float32), x_tiles,
                             precision=lax.Precision.HIGHEST)
        product = product * mask_block[:, None, None]
        return running.at[row_block].add(product), None

    aggregated = lax.scan(forward_step, jnp.zeros((NODES // TILE, TILE, H), jnp.float32), items)[0]
    hidden = aggregated.reshape(NODES, H).astype(jnp.bfloat16)
    preact = jnp.dot(hidden, weight, preferred_element_type=jnp.float32)
    sigma_pre = jax.nn.sigmoid(preact)
    layer_out = (preact * sigma_pre).astype(jnp.bfloat16)
    act_grad = (cotangent.astype(jnp.float32) * sigma_pre * (1.0 + preact * (1.0 - sigma_pre))).astype(jnp.bfloat16)
    weight_grad = jnp.dot(hidden.T, act_grad, preferred_element_type=jnp.float32) * (float(NODES) ** -0.5)
    hidden_grad = jnp.dot(act_grad, weight.T, preferred_element_type=jnp.float32).astype(jnp.bfloat16)
    grad_tiles_all = hidden_grad.reshape(NODES // TILE, TILE, H)

    def backward_step(running, batch):
        tile_block, row_block, col_block, mask_block = batch
        y_tiles = grad_tiles_all[row_block].astype(jnp.float32)
        product = jnp.einsum("gab,gah->gbh", tile_block.astype(jnp.float32), y_tiles,
                             precision=lax.Precision.HIGHEST)
        product = product * mask_block[:, None, None]
        return running.at[col_block].add(product), None

    gathered = lax.scan(backward_step, jnp.zeros((NODES // TILE, TILE, H), jnp.float32), items)[0]
    feature_grad = gathered.reshape(NODES, H).astype(jnp.bfloat16)
    return (layer_out, weight_grad, feature_grad)
```

```python
import functools

import jax
import jax.numpy as jnp
from jax import lax
from jax.experimental import pallas as pl
from jax.experimental.pallas import tpu as pltpu
from jax.sharding import PartitionSpec as P

F32 = jnp.float32
BF16 = jnp.bfloat16
MESH = pl.DeviceIdType.MESH
N = 256
A = 128
B = 128
DIST = (4, 3, -3, 2, -2, 1, -1, 0)
SEMS = dict(
    feat=8, core=8, xrow=8, ringz=16, ringx=8, xfin=1,
    own=8, part=8, xv=1, xu=8, pair=8,
    w1=8, w2=8, w3=4, w4=8, w5=8, grad=8,
)
OFFSET = {}
TOTAL = 0
for _name, _count in SEMS.items():
    OFFSET[_name] = TOTAL
    TOTAL += _count


def kernel(
    inv, feat, tiles_hbm, weight, cot,
    layer_out, weight_grad, feature_grad,
    tiles, xpan, pf, ks, kr, sxs, sx, rx, zs, rz, qs, rq, xfs, xfr, zf,
    hp, acc, w1s, w1r, w2s, w2r, w3r, w4r, w5r, gs, gr,
    ssem, rsem, tsem,
):
    r = lax.axis_index("row")
    c = lax.axis_index("col")
    xh, y = r // 4, r % 4
    xl, z, k = c // 16, (c % 16) // 2, c % 2
    ox, ok = 1 - xl, 1 - k

    def row_of(i):
        return ((xh + i // 4) % 2) * 4 + (y + i % 4) % 4

    def row_from(i):
        return ((xh + i // 4) % 2) * 4 + (y + 4 - i % 4) % 4

    def at_row(i):
        return (row_of(i), c)

    def at_z(d):
        return (r, xl * 16 + ((z + d + 8) % 8) * 2 + k)

    def at_x():
        return (r, ox * 16 + z * 2 + k)

    def at_core():
        return (r, xl * 16 + z * 2 + ok)

    def at_mate(i):
        return (r, ((xl + i // 2) % 2) * 16 + z * 2 + (k + i % 2) % 2)

    sent = []

    def desc(src, dst, name, i, to):
        return pltpu.make_async_remote_copy(
            src_ref=src, dst_ref=dst, send_sem=ssem.at[OFFSET[name] + i],
            recv_sem=rsem.at[OFFSET[name] + i], device_id=to, device_id_type=MESH,
        )

    def send(src, dst, name, i, to):
        d = desc(src, dst, name, i, to)
        d.start()
        sent.append(d)

    def arrive(dst, name, i):
        desc(dst, dst, name, i, at_core()).wait_recv()

    load = pltpu.make_async_copy(tiles_hbm, tiles.at[pl.ds(0, 192)], tsem)
    load.start()
    barrier = pltpu.get_barrier_semaphore()
    for i in range(1, 8):
        pl.semaphore_signal(barrier, inc=1, device_id=at_row(i), device_id_type=MESH)
        pl.semaphore_signal(barrier, inc=1, device_id=at_z(i), device_id_type=MESH)
    for i in range(1, 4):
        pl.semaphore_signal(barrier, inc=1, device_id=at_mate(i), device_id_type=MESH)
    tiles[192] = jnp.zeros((128, 128), BF16)
    xpan[r] = feat[...]
    pl.semaphore_wait(barrier, 17)

    for i in (4, 1, 3, 2, 5, 7, 6):
        send(feat, xpan.at[r], "feat", i, at_row(i))
    load.wait()
    for i in (4, 1, 3, 2, 5, 7, 6):
        arrive(xpan.at[row_from(i)], "feat", i)

    def forward(g):
        zt = (z + DIST[g] + 8) % 8

        @pl.loop(0, 2)
        def _(h):
            kt = ok + h * (2 * k - 1)
            total = None
            for p in range(8):
                rows = []
                for q in range(4):
                    cell = (2 * ((q // 2) * 16 + zt * 2 + kt) + q % 2) * 16 + 2 * p
                    rows.append(jnp.concatenate([tiles[inv[cell]], tiles[inv[cell + 1]]], axis=1))
                part = jnp.dot(jnp.concatenate(rows, axis=0), xpan[p], preferred_element_type=F32)
                total = part if total is None else total + part
            pf[g % 2, h] = total

        for q in range(2):
            ks[g, q] = pf[g % 2, 0, pl.ds(q * N, N)].astype(BF16)
        send(ks.at[g], kr.at[g], "core", g, at_core())

    def way(d):
        return (0, 4 - d) if d > 0 else (1, 4 + d)

    def process_z(g):
        d, par = DIST[g], g % 2
        arrive(kr.at[g], "core", g)
        sxs[g] = (pf[par, 1, pl.ds(ox * N, A)] + kr[g, ox, 0:A].astype(F32)).astype(BF16)
        send(sxs.at[g], rx.at[g], "xrow", g, at_x())
        if d != 0:
            for q in range(2):
                s = pf[par, 1, pl.ds(q * N + A, N - A)] + kr[g, q, A:N].astype(F32)
                if d == 4:
                    w, step = q, 0
                else:
                    w, step = way(d)
                    if step > 1 or q == w:
                        arrive(rz.at[w, step - 1, q], "ringz", (w * 4 + step - 1) * 2 + q)
                        s = s + rz[w, step - 1, q].astype(F32)
                zs[g, q] = s.astype(BF16)
                send(zs.at[g, q], rz.at[w, step, q], "ringz", (w * 4 + step) * 2 + q, at_z(1 - 2 * w))
        sx[g] = pf[par, 1, pl.ds(xl * N, A)] + kr[g, xl, 0:A].astype(F32)

    def process_x(g):
        d = DIST[g]
        arrive(rx.at[g], "xrow", g)
        s = sx[g] + rx[g].astype(F32)
        if d == 4:
            qs[g] = s.astype(BF16)
            for w in range(2):
                rows = pl.ds(w * (A // 2), A // 2)
                send(qs.at[g, rows], rq.at[w, 0, rows], "ringx", w * 4, at_z(1 - 2 * w))
            return
        w, step = way(d)
        if step == 1:
            rows = pl.ds(w * (A // 2), A // 2)
            arrive(rq.at[w, 0, rows], "ringx", w * 4)
            sx[g] = s
            sx[g, rows] += rq[w, 0, rows].astype(F32)
            s = sx[g]
        else:
            arrive(rq.at[w, step - 1], "ringx", w * 4 + step - 1)
            s = s + rq[w, step - 1].astype(F32)
        qs[g] = s.astype(BF16)
        send(qs.at[g], rq.at[w, step], "ringx", w * 4 + step, at_z(1 - 2 * w))

    forward(0)
    process_z(0)
    forward(1)
    forward(2)
    process_z(1)
    process_z(2)
    process_x(0)
    forward(3)
    process_x(1)
    process_x(2)
    forward(4)
    process_z(3)
    process_z(4)
    forward(5)
    process_x(3)
    process_x(4)
    forward(6)
    process_z(5)
    process_z(6)
    forward(7)
    process_x(5)
    process_x(6)
    process_z(7)
    for w in range(2):
        for q in range(2):
            arrive(rz.at[w, 3, q], "ringz", (w * 4 + 3) * 2 + q)
    xfs[...] = (
        pf[1, 1, pl.ds(ox * N + A, N - A)] + kr[7, ox, A:N].astype(F32)
        + rz[0, 3, ox].astype(F32) + rz[1, 3, ox].astype(F32)
    ).astype(BF16)
    send(xfs, xfr, "xfin", 0, at_x())
    zf[...] = (
        pf[1, 1, pl.ds(xl * N + A, N - A)] + kr[7, xl, A:N].astype(F32)
        + rz[0, 3, xl].astype(F32) + rz[1, 3, xl].astype(F32)
    )
    arrive(rx.at[7], "xrow", 7)
    for w in range(2):
        arrive(rq.at[w, 3], "ringx", w * 4 + 3)
    head = (sx[7] + rx[7].astype(F32) + rq[0, 3].astype(F32) + rq[1, 3].astype(F32)).astype(BF16)
    arrive(xfr, "xfin", 0)
    tail = (zf[...] + xfr[...].astype(F32)).astype(BF16)

    hidden = jnp.concatenate([head, tail], axis=0)
    preact = jnp.dot(hidden, weight[...], preferred_element_type=F32)
    sig = jax.nn.sigmoid(preact)
    layer_out[...] = (preact * sig).astype(BF16)
    act = (cot[...].astype(F32) * sig * (1.0 + preact * (1.0 - sig))).astype(BF16)
    hp[z, k, xl] = jnp.dot(act, weight[...].T, preferred_element_type=F32).astype(BF16)

    head_rows, tail_rows = pl.ds(0, B), pl.ds(B, N - B)
    mine = hp.at[z, k, xl]
    send(mine.at[tail_rows], mine.at[tail_rows], "xv", 0, at_x())
    send(mine, mine, "own", 0, at_z(1))
    send(mine, mine, "own", 4, at_z(-1))
    send(mine.at[head_rows], mine.at[head_rows], "xu", 0, at_x())

    w1s[...] = jnp.dot(hidden.T, act, preferred_element_type=F32).reshape(8, 32, N)
    for i in range(1, 8):
        send(w1s.at[row_of(i)], w1r.at[r], "w1", i, at_row(i))
    acc[...] = jnp.zeros_like(acc)

    def place(d):
        return (z + d + 8) % 8

    def came_from(w, step):
        return place(-1 - step) if w == 0 else place(1 + step)

    def number(d):
        return d if d >= 0 else 8 + d

    def own_step(w, step):
        to = at_z(1 - 2 * w)
        dist = -1 - step if w == 0 else 1 + step
        block = hp.at[came_from(w, step), k, xl]
        if step < 3:
            arrive(block, "own", w * 4 + step)
            if step < 2:
                send(block, block, "own", w * 4 + step + 1, to)
            else:
                half = block.at[pl.ds(w * 128, 128)]
                send(half, half, "own", w * 4 + 3, to)
            send(block.at[head_rows], block.at[head_rows], "xu", number(dist), at_x())
        else:
            half = block.at[pl.ds(w * 128, 128)]
            arrive(half, "own", w * 4 + 3)
            if w == 0:
                send(half, half, "xu", 4, at_x())

    def part_step(w, step):
        to = at_z(1 - 2 * w)
        block = hp.at[came_from(w, step), k, ox]
        rows = block.at[tail_rows] if step < 3 else block.at[pl.ds(B + w * 64, 64)]
        arrive(rows, "part", w * 4 + step)
        if step < 2:
            send(rows, rows, "part", w * 4 + step + 1, to)
        elif step == 2:
            half = block.at[pl.ds(B + w * 64, 64)]
            send(half, half, "part", w * 4 + 3, to)

    def share(d):
        block = hp.at[place(d), k, ox, head_rows]
        arrive(block, "xu", number(d))
        both = hp.at[place(d), k]
        send(both, both, "pair", number(d), at_core())

    def have(d):
        arrive(hp.at[place(d), ok], "pair", number(d))

    def backward(d, first, last):
        zt = place(d)
        left = jnp.concatenate([hp[zt, q // 2, q % 2] for q in range(4)], axis=0).T

        @pl.loop(first, last)
        def _(n):
            acc[n] += jnp.dot(left, right_of(zt, n), preferred_element_type=F32)

    def right_of(zt, n):
        rows = []
        for q in range(8):
            block = ((q // 2) % 2) * 16 + zt * 2 + q // 4
            cell = (2 * block + q % 2) * 16 + 2 * n
            rows.append(jnp.concatenate([tiles[inv[cell]], tiles[inv[cell + 1]]], axis=1))
        return jnp.concatenate(rows, axis=0)

    arrive(hp.at[z, k, ox, tail_rows], "xv", 0)
    block = hp.at[z, k, ox, tail_rows]
    send(block, block, "part", 0, at_z(1))
    send(block, block, "part", 4, at_z(-1))
    share(0)
    own_step(0, 0)
    own_step(1, 0)
    have(0)
    backward(0, 0, 4)
    part_step(0, 0)
    part_step(1, 0)
    backward(0, 4, 8)
    for i in range(1, 8):
        arrive(w1r.at[row_from(i)], "w1", i)
    w1r[r] = w1s[r]
    s = w1r[0]
    for i in range(1, 8):
        s = s + w1r[i]
    for i in range(8):
        w2s[i] = s[(i // 2) * 8:(i // 2) * 8 + 8, (i % 2) * 128:(i % 2) * 128 + 128]
    for i in range(1, 8):
        send(w2s.at[place(i)], w2r.at[z], "w2", i, at_z(i))
    share(-1)
    share(1)
    own_step(0, 1)
    own_step(1, 1)
    have(-1)
    backward(-1, 0, 4)
    part_step(0, 1)
    part_step(1, 1)
    backward(-1, 4, 8)
    have(1)
    backward(1, 0, 8)
    for i in range(1, 8):
        arrive(w2r.at[place(-i)], "w2", i)
    w2r[z] = w2s[z]
    s = w2r[0]
    for i in range(1, 8):
        s = s + w2r[i]
    w3r[xl * 2 + k] = s
    for i in range(1, 4):
        send(w3r.at[xl * 2 + k], w3r.at[xl * 2 + k], "w3", i, at_mate(i))
    share(-2)
    own_step(0, 2)
    own_step(1, 2)
    share(2)
    have(-2)
    backward(-2, 0, 4)
    part_step(0, 2)
    part_step(1, 2)
    backward(-2, 4, 8)
    for i in range(1, 4):
        arrive(w3r.at[((xl + i // 2) % 2) * 2 + (k + i % 2) % 2], "w3", i)
    w4r[z] = (w3r[0] + w3r[1]) + (w3r[2] + w3r[3])
    for i in range(1, 8):
        send(w4r.at[z], w4r.at[z], "w4", i, at_z(i))
    have(2)
    backward(2, 0, 4)
    own_step(0, 3)
    backward(2, 4, 8)
    share(-3)
    share(3)
    have(-3)
    backward(-3, 0, 8)
    own_step(1, 3)
    part_step(0, 3)
    part_step(1, 3)
    share(4)
    for i in range(1, 8):
        arrive(w4r.at[place(-i)], "w4", i)
    for i in range(8):
        w5r[r, (i // 2) * 8:(i // 2) * 8 + 8, (i % 2) * 128:(i % 2) * 128 + 128] = w4r[i]
    for i in range(1, 8):
        send(w5r.at[r], w5r.at[r], "w5", i, at_row(i))
    have(3)
    backward(3, 0, 8)
    have(4)

    zt = place(4)
    left = jnp.concatenate([hp[zt, q // 2, q % 2] for q in range(4)], axis=0).T

    @pl.loop(0, 8)
    def _(j):
        i = (j + 1) % 8
        n = row_of(i)
        acc[n] += jnp.dot(left, right_of(zt, n), preferred_element_type=F32)

        @pl.when(i != 0)
        def _():
            gs[n] = acc[n].astype(BF16)
            desc(gs.at[n], gr.at[r], "grad", i, at_row(i)).start()

    for i in range(1, 8):
        arrive(w5r.at[row_from(i)], "w5", i)
    weight_grad[...] = w5r[...].reshape(N, N) * (65536.0 ** -0.5)
    s = acc[r]
    for i in range(1, 8):
        arrive(gr.at[row_from(i)], "grad", i)
        s = s + gr[row_from(i)].astype(F32)
    feature_grad[...] = s.T.astype(BF16)
    for d in sent:
        d.wait_send()
    for i in range(1, 8):
        desc(gs.at[row_of(i)], gr.at[r], "grad", i, at_row(i)).wait_send()


def body(features, edge_tiles, tile_slot, tile_count, weight, cotangent):
    slots = tile_slot.reshape(192)
    ids = jnp.arange(192, dtype=jnp.int32)
    slots = jnp.where(ids < tile_count.reshape(()), slots, -1)
    cells = jnp.arange(1024, dtype=jnp.int32)
    hit = slots[None, :] == cells[:, None]
    inv = 192 + jnp.sum(jnp.where(hit, ids[None, :] - 192, 0), axis=1, dtype=jnp.int32)
    vmem = pl.BlockSpec(memory_space=pltpu.VMEM)

    def buf(*shape, dtype=BF16):
        return pltpu.VMEM(shape, dtype)

    return pl.pallas_call(
        kernel,
        out_shape=(
            jax.ShapeDtypeStruct((N, N), BF16),
            jax.ShapeDtypeStruct((N, N), F32),
            jax.ShapeDtypeStruct((N, N), BF16),
        ),
        in_specs=[pl.BlockSpec(memory_space=pltpu.SMEM), vmem, pl.BlockSpec(memory_space=pl.ANY), vmem, vmem],
        out_specs=(vmem, vmem, vmem),
        scratch_shapes=[
            buf(193, 128, 128),
            buf(8, N, N),
            buf(2, 2, 2 * N, N, dtype=F32),
            buf(8, 2, N, N),
            buf(8, 2, N, N),
            buf(8, A, N),
            buf(8, A, N, dtype=F32),
            buf(8, A, N),
            buf(7, 2, N - A, N),
            buf(2, 4, 2, N - A, N),
            buf(7, A, N),
            buf(2, 4, A, N),
            buf(N - A, N),
            buf(N - A, N),
            buf(N - A, N, dtype=F32),
            buf(8, 2, 2, N, N),
            buf(8, N, N, dtype=F32),
            buf(8, 32, N, dtype=F32),
            buf(8, 32, N, dtype=F32),
            buf(8, 8, 128, dtype=F32),
            buf(8, 8, 128, dtype=F32),
            buf(4, 8, 128, dtype=F32),
            buf(8, 8, 128, dtype=F32),
            buf(8, 32, N, dtype=F32),
            buf(8, N, N),
            buf(8, N, N),
            pltpu.SemaphoreType.DMA((TOTAL,)),
            pltpu.SemaphoreType.DMA((TOTAL,)),
            pltpu.SemaphoreType.DMA,
        ],
        compiler_params=pltpu.CompilerParams(
            collective_id=0, has_side_effects=True, vmem_limit_bytes=56 * 2**20
        ),
    )(inv, features, edge_tiles.reshape(192, 128, 128), weight, cotangent)


def solution(mesh):
    in_specs = (
        P(("col", "row"), None),
        P("row", "col", None, None),
        P("row", "col"),
        P("row", "col"),
        P(),
        P(("row", "col"), None),
    )
    out_specs = (P(("row", "col"), None), P(), P(("col", "row"), None))
    return jax.shard_map(body, mesh=mesh, in_specs=in_specs, out_specs=out_specs, check_vma=False)
```

```python
import functools

import jax
import jax.numpy as jnp
from jax import lax
from jax.experimental import pallas as pl
from jax.experimental.pallas import tpu as pltpu
from jax.sharding import PartitionSpec as P

F32 = jnp.float32
BF16 = jnp.bfloat16
MESH = pl.DeviceIdType.MESH
N = 256
A = 128
B = 128
DIST = (4, 3, -3, 2, -2, 1, -1, 0)
SEMS = dict(
    feat=8, core=8, xrow=8, ringz=16, ringx=8, xfin=1,
    head=8, tail=8, part=8, xv=1, xu=8, pair=8,
    w1=8, w2=8, w3=4, w4=8, w5=8, grad=8,
)
SUMS = (
    "Fa0", "Fb0", "Fa1", "Fb1", "S0", "Z00", "Z01", "Fa2", "S1", "Z11", "Fb2", "Fa3", "S2", "Z20", "Fb3", "X0", "Z10",
    "Z21", "S3", "Fa4", "Fb4", "Z31", "Fa5", "S4", "Z40", "X1", "Fb5", "X2", "S5", "Z30", "Fa6", "Z41", "Fb6", "Z51",
    "Fa7", "S6", "Z60", "X3", "Fb7", "X4", "S7", "Z50", "Z61", "X5", "X6", "P0", "P1", "P2", "P3",
)
GATHER = (
    "W1", "OH00", "OH10", "V", "SH0", "OT10", "OT00", "C0,0", "OH01", "OH11", "C0,1", "C0,2", "C0,3", "PT10", "PT00",
    "SH-1", "W2", "OT01", "OT11", "SH1", "C-1,0", "C-1,1", "OH12", "OH02", "C-1,2", "C-1,3", "PT01", "SH-2", "PT11",
    "SH2", "C1,0", "C1,1", "OT02", "OT12", "C1,2", "W3", "C1,3", "OH03", "C-2,0", "C-2,1", "PT12", "PT02", "SH3",
    "SH-3", "C-2,2", "C-2,3", "OT13", "W4", "C2,0", "C2,1", "C2,2", "PT13", "PT03", "SH4", "C2,3", "C-3,0", "C-3,1",
    "C-3,2", "C-3,3", "C3,0", "W5", "C3,1", "C3,2", "C3,3",
)
OFFSET = {}
TOTAL = 0
for _name, _count in SEMS.items():
    OFFSET[_name] = TOTAL
    TOTAL += _count


def kernel(
    slots, count, feat, tiles_hbm, weight_hbm, cot_hbm,
    layer_out, weight_grad, feature_grad,
    tiles, xpan, pacc, ks, kr, sxs, sx, rx, zs, rz, qs, rq, xfs, xfr, zf,
    hp, lt, acc, w1s, w1r, w2s, w2r, w3r, w4r, w5r, gs, gr, weight, cot, inv_v, inv,
    ssem, rsem, tsem,
):
    r = lax.axis_index("row")
    c = lax.axis_index("col")
    xh, y = r // 4, r % 4
    xl, z, k = c // 16, (c % 16) // 2, c % 2
    ox, ok = 1 - xl, 1 - k

    def row_of(i):
        return ((xh + i // 4) % 2) * 4 + (y + i % 4) % 4

    def row_from(i):
        return ((xh + i // 4) % 2) * 4 + (y + 4 - i % 4) % 4

    def at_row(i):
        return (row_of(i), c)

    def at_z(d):
        return (r, xl * 16 + ((z + d + 8) % 8) * 2 + k)

    def at_x():
        return (r, ox * 16 + z * 2 + k)

    def at_core():
        return (r, xl * 16 + z * 2 + ok)

    def at_mate(i):
        return (r, ((xl + i // 2) % 2) * 16 + z * 2 + (k + i % 2) % 2)

    sent = []

    def desc(src, dst, name, i, to):
        return pltpu.make_async_remote_copy(
            src_ref=src, dst_ref=dst, send_sem=ssem.at[OFFSET[name] + i],
            recv_sem=rsem.at[OFFSET[name] + i], device_id=to, device_id_type=MESH,
        )

    def send(src, dst, name, i, to):
        d = desc(src, dst, name, i, to)
        d.start()
        sent.append(d)

    def arrive(dst, name, i):
        desc(dst, dst, name, i, at_core()).wait_recv()

    barrier = pltpu.get_barrier_semaphore()
    for i in range(1, 8):
        pl.semaphore_signal(barrier, inc=1, device_id=at_row(i), device_id_type=MESH)
        pl.semaphore_signal(barrier, inc=1, device_id=at_z(i), device_id_type=MESH)
    for i in range(1, 4):
        pl.semaphore_signal(barrier, inc=1, device_id=at_mate(i), device_id_type=MESH)
    local = [
        pltpu.make_async_copy(src, dst, tsem.at[i])
        for i, (src, dst) in enumerate((
            (feat, xpan.at[r]), (tiles_hbm, tiles.at[pl.ds(0, 192)]), (weight_hbm, weight), (cot_hbm, cot),
        ))
    ]
    for copy in local:
        copy.start()
    tiles[192] = jnp.zeros((128, 128), BF16)
    cell = lax.broadcasted_iota(jnp.int32, (8, 128), 0) * 128 + lax.broadcasted_iota(jnp.int32, (8, 128), 1)
    live = count[0, 0]

    def find(s, table):
        return jnp.where((cell == slots[0, s]) & (s < live), s, table)

    inv_v[...] = lax.fori_loop(0, 192, find, jnp.full((8, 128), 192, jnp.int32), unroll=8)
    place_table = pltpu.make_async_copy(inv_v, inv, tsem.at[4])
    place_table.start()
    local[0].wait()
    pl.semaphore_wait(barrier, 17)

    for i in (4, 1, 3, 2, 5, 7, 6):
        send(xpan.at[r], xpan.at[r], "feat", i, at_row(i))
    place_table.wait()
    local[1].wait()

    def pair(row, p):
        n, at = row // 8, (row % 8) * 16 + 2 * p
        return jnp.concatenate([tiles[inv[n, at]], tiles[inv[n, at + 1]]], axis=1)

    def product(zt, kt, blocks):
        total = None
        for p in blocks:
            rows = [pair(2 * ((q // 2) * 16 + zt * 2 + kt) + q % 2, p) for q in range(4)]
            part = jnp.dot(jnp.concatenate(rows, axis=0), xpan[p], preferred_element_type=F32)
            total = part if total is None else total + part
        return total

    @pl.loop(0, 16)
    def _(j):
        pacc[j // 2, j % 2] = product(j // 2, j % 2, [r])

    for i in (1, 3, 4):
        arrive(xpan.at[row_from(i)], "feat", i)

    @pl.loop(0, 16)
    def _(j):
        pacc[j // 2, j % 2] += product(j // 2, j % 2, [row_from(i) for i in (1, 3, 4)])

    for i in (2, 5, 7, 6):
        arrive(xpan.at[row_from(i)], "feat", i)

    def side(q):
        return xl if q else ox

    def forward(g, h):
        zt = (z + DIST[g] + 8) % 8
        kt = k if h else ok
        pacc[zt, kt] += product(zt, kt, [row_from(i) for i in (2, 5, 7, 6)])
        if h == 0:
            for q in range(2):
                ks[g, q] = pacc[zt, kt, pl.ds(q * N, N)].astype(BF16)
            send(ks.at[g], kr.at[g], "core", g, at_core())

    def chip_sum(g, q, first, last):
        zt, x = (z + DIST[g] + 8) % 8, side(q)
        return pacc[zt, k, pl.ds(x * N + first, last - first)] + kr[g, x, first:last].astype(F32)

    def way(d):
        return (0, 4 - d) if d > 0 else (1, 4 + d)

    def chip(g):
        arrive(kr.at[g], "core", g)
        sxs[g] = chip_sum(g, 0, 0, A).astype(BF16)
        send(sxs.at[g], rx.at[g], "xrow", g, at_x())
        sx[g] = chip_sum(g, 1, 0, A)

    def ring_z(g, q):
        s = chip_sum(g, q, A, N)
        w, step = (q, 0) if DIST[g] == 4 else way(DIST[g])
        if step > 1 or (step == 1 and q == w):
            arrive(rz.at[w, step - 1, q], "ringz", (w * 4 + step - 1) * 2 + q)
            s = s + rz[w, step - 1, q].astype(F32)
        zs[g, q] = s.astype(BF16)
        send(zs.at[g, q], rz.at[w, step, q], "ringz", (w * 4 + step) * 2 + q, at_z(1 - 2 * w))

    def ring_x(g):
        d = DIST[g]
        arrive(rx.at[g], "xrow", g)
        s = sx[g] + rx[g].astype(F32)
        if d == 4:
            qs[g] = s.astype(BF16)
            for w in range(2):
                rows = pl.ds(w * (A // 2), A // 2)
                send(qs.at[g, rows], rq.at[w, 0, rows], "ringx", w * 4, at_z(1 - 2 * w))
            return
        w, step = way(d)
        if step == 1:
            rows = pl.ds(w * (A // 2), A // 2)
            arrive(rq.at[w, 0, rows], "ringx", w * 4)
            sx[g] = s
            sx[g, rows] += rq[w, 0, rows].astype(F32)
            s = sx[g]
        else:
            arrive(rq.at[w, step - 1], "ringx", w * 4 + step - 1)
            s = s + rq[w, step - 1].astype(F32)
        qs[g] = s.astype(BF16)
        send(qs.at[g], rq.at[w, step], "ringx", w * 4 + step, at_z(1 - 2 * w))

    def last_z(q):
        for w in range(2):
            arrive(rz.at[w, 3, q], "ringz", (w * 4 + 3) * 2 + q)
        s = chip_sum(7, q, A, N) + rz[0, 3, q].astype(F32) + rz[1, 3, q].astype(F32)
        if q == 0:
            xfs[...] = s.astype(BF16)
            send(xfs, xfr, "xfin", 0, at_x())
        else:
            zf[...] = s

    for op in SUMS:
        if op[:2] == "Fa":
            forward(int(op[2]), 0)
        elif op[:2] == "Fb":
            forward(int(op[2]), 1)
        elif op[0] == "S":
            chip(int(op[1]))
        elif op[0] == "Z":
            ring_z(int(op[1]), int(op[2]))
        elif op[0] == "X":
            ring_x(int(op[1]))
        elif op in ("P0", "P1"):
            last_z(int(op[1]))
    arrive(rx.at[7], "xrow", 7)
    for w in range(2):
        arrive(rq.at[w, 3], "ringx", w * 4 + 3)
    head = (sx[7] + rx[7].astype(F32) + rq[0, 3].astype(F32) + rq[1, 3].astype(F32)).astype(BF16)
    arrive(xfr, "xfin", 0)
    tail = (zf[...] + xfr[...].astype(F32)).astype(BF16)
    local[2].wait()
    local[3].wait()

    hidden = jnp.concatenate([head, tail], axis=0)
    preact = jnp.dot(hidden, weight[...], preferred_element_type=F32)
    sig = jax.nn.sigmoid(preact)
    layer_out[...] = (preact * sig).astype(BF16)
    act = (cot[...].astype(F32) * sig * (1.0 + preact * (1.0 - sig))).astype(BF16)
    hp[z, k, xl] = jnp.dot(act, weight[...].T, preferred_element_type=F32).astype(BF16)

    head_rows, tail_rows = pl.ds(0, B), pl.ds(B, N - B)
    mine = hp.at[z, k, xl]
    mine_head, mine_tail = mine.at[head_rows], mine.at[tail_rows]
    send(mine_tail, mine_tail, "xv", 0, at_x())
    send(mine_head, mine_head, "head", 0, at_z(1))
    send(mine_head, mine_head, "head", 4, at_z(-1))
    send(mine_head, mine_head, "xu", 0, at_x())
    send(mine_tail, mine_tail, "tail", 0, at_z(1))
    send(mine_tail, mine_tail, "tail", 4, at_z(-1))

    def place(d):
        return (z + d + 8) % 8

    def came_from(w, step):
        return place(-1 - step) if w == 0 else place(1 + step)

    def number(d):
        return d if d >= 0 else 8 + d

    def head_step(w, step):
        dist = 4 if step == 3 else (1 + step if w else -1 - step)
        rows = hp.at[came_from(w, step), k, xl, head_rows]
        arrive(rows, "head", w * 4 + step)
        if step < 2 or (step == 2 and w == 0):
            send(rows, rows, "head", w * 4 + step + 1, at_z(1 - 2 * w))
        send(rows, rows, "xu", number(dist), at_x())

    def tail_step(w, step):
        rows = hp.at[came_from(w, step), k, xl, tail_rows]
        arrive(rows, "tail", w * 4 + step)
        if step < 2 or (step == 2 and w == 1):
            send(rows, rows, "tail", w * 4 + step + 1, at_z(1 - 2 * w))

    def part_step(w, step):
        to = at_z(1 - 2 * w)
        block = hp.at[came_from(w, step), k, ox]
        rows = block.at[tail_rows] if step < 3 else block.at[pl.ds(B + w * 64, 64)]
        arrive(rows, "part", w * 4 + step)
        if step < 2:
            send(rows, rows, "part", w * 4 + step + 1, to)
        elif step == 2:
            half = block.at[pl.ds(B + w * 64, 64)]
            send(half, half, "part", w * 4 + 3, to)

    def share(d):
        block = hp.at[place(d), k, ox, head_rows]
        arrive(block, "xu", number(d))
        both = hp.at[place(d), k]
        send(both, both, "pair", number(d), at_core())

    def have(d):
        arrive(hp.at[place(d), ok], "pair", number(d))
        lt[...] = jnp.concatenate([hp[place(d), q // 2, q % 2] for q in range(4)], axis=0).T

    def add_product(d, n):
        rows = [pair(2 * (((q // 2) % 2) * 16 + place(d) * 2 + q // 4) + q % 2, n) for q in range(8)]
        acc[n] += jnp.dot(lt[...], jnp.concatenate(rows, axis=0), preferred_element_type=F32)

    def backward(d, part):
        if part == 0:
            have(d)

        @pl.loop(2 * part, 2 * part + 2)
        def _(n):
            add_product(d, n)

    def x_tail():
        rows = hp.at[z, k, ox, tail_rows]
        arrive(rows, "xv", 0)
        send(rows, rows, "part", 0, at_z(1))
        send(rows, rows, "part", 4, at_z(-1))

    def gradient_step(step):
        if step == 1:
            w1s[...] = jnp.dot(hidden.T, act, preferred_element_type=F32).reshape(8, 32, N)
            for i in range(1, 8):
                send(w1s.at[row_of(i)], w1r.at[r], "w1", i, at_row(i))
            acc[...] = jnp.zeros_like(acc)
        elif step == 2:
            for i in range(1, 8):
                arrive(w1r.at[row_from(i)], "w1", i)
            w1r[r] = w1s[r]
            s = w1r[0]
            for i in range(1, 8):
                s = s + w1r[i]
            for i in range(8):
                w2s[i] = s[(i // 2) * 8:(i // 2) * 8 + 8, (i % 2) * 128:(i % 2) * 128 + 128]
            for i in range(1, 8):
                send(w2s.at[place(i)], w2r.at[z], "w2", i, at_z(i))
        elif step == 3:
            for i in range(1, 8):
                arrive(w2r.at[place(-i)], "w2", i)
            w2r[z] = w2s[z]
            s = w2r[0]
            for i in range(1, 8):
                s = s + w2r[i]
            w3r[xl * 2 + k] = s
            for i in range(1, 4):
                send(w3r.at[xl * 2 + k], w3r.at[xl * 2 + k], "w3", i, at_mate(i))
        elif step == 4:
            for i in range(1, 4):
                arrive(w3r.at[((xl + i // 2) % 2) * 2 + (k + i % 2) % 2], "w3", i)
            w4r[z] = (w3r[0] + w3r[1]) + (w3r[2] + w3r[3])
            for i in range(1, 8):
                send(w4r.at[z], w4r.at[z], "w4", i, at_z(i))
        else:
            for i in range(1, 8):
                arrive(w4r.at[place(-i)], "w4", i)
            for i in range(8):
                w5r[r, (i // 2) * 8:(i // 2) * 8 + 8, (i % 2) * 128:(i % 2) * 128 + 128] = w4r[i]
            for i in range(1, 8):
                send(w5r.at[r], w5r.at[r], "w5", i, at_row(i))

    for op in GATHER:
        if op[:2] == "OH":
            head_step(int(op[2]), int(op[3]))
        elif op[:2] == "OT":
            tail_step(int(op[2]), int(op[3]))
        elif op[:2] == "PT":
            part_step(int(op[2]), int(op[3]))
        elif op[:2] == "SH":
            share(int(op[2:]))
        elif op[0] == "C":
            d, part = op[1:].split(",")
            backward(int(d), int(part))
        elif op[0] == "W":
            gradient_step(int(op[1]))
        else:
            x_tail()

    have(4)

    @pl.loop(0, 8)
    def _(j):
        i = (j + 1) % 8
        n = row_of(i)
        add_product(4, n)

        @pl.when(i != 0)
        def _():
            gs[n] = acc[n].astype(BF16)
            desc(gs.at[n], gr.at[r], "grad", i, at_row(i)).start()

    for i in range(1, 8):
        arrive(w5r.at[row_from(i)], "w5", i)
    weight_grad[...] = w5r[...].reshape(N, N) * (65536.0 ** -0.5)
    s = acc[r]
    for i in range(1, 8):
        arrive(gr.at[row_from(i)], "grad", i)
        s = s + gr[row_from(i)].astype(F32)
    feature_grad[...] = s.T.astype(BF16)
    for d in sent:
        d.wait_send()
    for i in range(1, 8):
        desc(gs.at[row_of(i)], gr.at[r], "grad", i, at_row(i)).wait_send()


def hand_over(a, b, c, a_out, b_out, c_out):
    a_out[...] = a[...]
    b_out[...] = b[...]
    c_out[...] = c[...]


def body(features, edge_tiles, tile_slot, tile_count, weight, cotangent):
    vmem = pl.BlockSpec(memory_space=pltpu.VMEM)

    def buf(*shape, dtype=BF16):
        return pltpu.VMEM(shape, dtype)

    hbm = pl.BlockSpec(memory_space=pl.ANY)
    smem = pl.BlockSpec(memory_space=pltpu.SMEM)
    shapes = (
        jax.ShapeDtypeStruct((N, N), BF16),
        jax.ShapeDtypeStruct((N, N), F32),
        jax.ShapeDtypeStruct((N, N), BF16),
    )
    results = pl.pallas_call(
        kernel,
        out_shape=shapes,
        in_specs=[smem, smem, hbm, hbm, hbm, hbm],
        out_specs=(vmem, vmem, vmem),
        scratch_shapes=[
            buf(193, 128, 128),
            buf(8, N, N),
            buf(8, 2, 2 * N, N, dtype=F32),
            buf(8, 2, N, N),
            buf(8, 2, N, N),
            buf(8, A, N),
            buf(8, A, N, dtype=F32),
            buf(8, A, N),
            buf(7, 2, N - A, N),
            buf(2, 4, 2, N - A, N),
            buf(7, A, N),
            buf(2, 4, A, N),
            buf(N - A, N),
            buf(N - A, N),
            buf(N - A, N, dtype=F32),
            buf(8, 2, 2, N, N),
            buf(N, 4 * N),
            buf(8, N, N, dtype=F32),
            buf(8, 32, N, dtype=F32),
            buf(8, 32, N, dtype=F32),
            buf(8, 8, 128, dtype=F32),
            buf(8, 8, 128, dtype=F32),
            buf(4, 8, 128, dtype=F32),
            buf(8, 8, 128, dtype=F32),
            buf(8, 32, N, dtype=F32),
            buf(8, N, N),
            buf(8, N, N),
            buf(N, N),
            buf(N, N),
            buf(8, 128, dtype=jnp.int32),
            pltpu.SMEM((8, 128), jnp.int32),
            pltpu.SemaphoreType.DMA((TOTAL,)),
            pltpu.SemaphoreType.DMA((TOTAL,)),
            pltpu.SemaphoreType.DMA((5,)),
        ],
        compiler_params=pltpu.CompilerParams(
            collective_id=0, has_side_effects=True, vmem_limit_bytes=56 * 2**20
        ),
    )(tile_slot, tile_count, features, edge_tiles.reshape(192, 128, 128), weight, cotangent)
    return pl.pallas_call(
        hand_over,
        out_shape=shapes,
        in_specs=[vmem] * 3,
        out_specs=(vmem,) * 3,
    )(*results)


def solution(mesh):
    in_specs = (
        P(("col", "row"), None),
        P("row", "col", None, None),
        P("row", "col"),
        P("row", "col"),
        P(),
        P(("row", "col"), None),
    )
    out_specs = (P(("row", "col"), None), P(), P(("col", "row"), None))
    return jax.shard_map(body, mesh=mesh, in_specs=in_specs, out_specs=out_specs, check_vma=False)
```

```python
import functools

import jax
import jax.numpy as jnp
from jax import lax
from jax.experimental import pallas as pl
from jax.experimental.pallas import tpu as pltpu
from jax.sharding import PartitionSpec as P

F32 = jnp.float32
BF16 = jnp.bfloat16
MESH = pl.DeviceIdType.MESH
N = 256
A = 128
B = 128
DIST = (4, 3, -3, 2, -2, 1, -1, 0)
SEMS = dict(
    feat=8, core=8, xrow=8, ringz=16, ringx=8, xfin=1,
    head=8, tail=8, part=8, xv=1, xu=8, pair=8,
    w1=8, w2=8, w3=4, w4=8, w5=8, grad=8,
)
SUMS = (
    "Fa0", "Fb0", "Fa1", "Fb1", "S0", "Z00", "Z01", "Fa2", "S1", "Z11", "Fb2", "Fa3", "S2", "Z20", "Fb3", "X0", "Z10",
    "Z21", "S3", "Fa4", "Fb4", "Z31", "Fa5", "S4", "Z40", "X1", "Fb5", "X2", "S5", "Z30", "Fa6", "Z41", "Fb6", "Z51",
    "Fa7", "S6", "Z60", "X3", "Fb7", "X4", "S7", "Z50", "Z61", "X5", "X6", "P0", "P1", "P2", "P3",
)
GATHER = (
    "OH00", "OH10", "V", "W1", "SH0", "OT10", "OT00", "C0,0", "OH01", "OH11", "C0,1", "C0,2", "C0,3", "PT10", "PT00",
    "SH-1", "OT01", "OT11", "SH1", "C-1,0", "C-1,1", "OH12", "OH02", "W2", "C-1,2", "C-1,3", "PT01", "SH-2", "PT11",
    "SH2", "C1,0", "C1,1", "OT02", "OT12", "C1,2", "C1,3", "OH03", "C-2,0", "C-2,1", "PT12", "PT02", "SH3", "SH-3",
    "C-2,2", "C-2,3", "OT13", "C2,0", "C2,1", "C2,2", "PT13", "PT03", "SH4", "C2,3", "C-3,0", "C-3,1", "C-3,2",
    "C-3,3", "W3", "C3,0", "C3,1", "C3,2", "C3,3", "W4",
)
OFFSET = {}
TOTAL = 0
for _name, _count in SEMS.items():
    OFFSET[_name] = TOTAL
    TOTAL += _count


def kernel(
    slots, count, feat, tiles_hbm, weight_hbm, cot_hbm,
    layer_out, weight_grad, feature_grad,
    tiles, xpan, pacc, ks, kr, sxs, sx, rx, zs, rz, qs, rq, xfs, xfr, zf,
    hp, lt, acc, w1s, w1r, w2s, w2r, w3r, w4r, w5r, gs, gr, weight, cot, inv_v, inv,
    ssem, rsem, tsem,
):
    r = lax.axis_index("row")
    c = lax.axis_index("col")
    xh, y = r // 4, r % 4
    xl, z, k = c // 16, (c % 16) // 2, c % 2
    ox, ok = 1 - xl, 1 - k

    def row_of(i):
        return ((xh + i // 4) % 2) * 4 + (y + i % 4) % 4

    def row_from(i):
        return ((xh + i // 4) % 2) * 4 + (y + 4 - i % 4) % 4

    def at_row(i):
        return (row_of(i), c)

    def at_z(d):
        return (r, xl * 16 + ((z + d + 8) % 8) * 2 + k)

    def at_x():
        return (r, ox * 16 + z * 2 + k)

    def at_core():
        return (r, xl * 16 + z * 2 + ok)

    def at_mate(i):
        return (r, ((xl + i // 2) % 2) * 16 + z * 2 + (k + i % 2) % 2)

    sent = []

    def desc(src, dst, name, i, to):
        return pltpu.make_async_remote_copy(
            src_ref=src, dst_ref=dst, send_sem=ssem.at[OFFSET[name] + i],
            recv_sem=rsem.at[OFFSET[name] + i], device_id=to, device_id_type=MESH,
        )

    def send(src, dst, name, i, to):
        d = desc(src, dst, name, i, to)
        d.start()
        sent.append(d)

    def arrive(dst, name, i):
        desc(dst, dst, name, i, at_core()).wait_recv()

    barrier = pltpu.get_barrier_semaphore()
    for i in range(1, 8):
        pl.semaphore_signal(barrier, inc=1, device_id=at_row(i), device_id_type=MESH)
        pl.semaphore_signal(barrier, inc=1, device_id=at_z(i), device_id_type=MESH)
    for i in range(1, 4):
        pl.semaphore_signal(barrier, inc=1, device_id=at_mate(i), device_id_type=MESH)
    local = [
        pltpu.make_async_copy(src, dst, tsem.at[i])
        for i, (src, dst) in enumerate((
            (feat, xpan.at[r]), (tiles_hbm, tiles.at[pl.ds(0, 192)]), (weight_hbm, weight), (cot_hbm, cot),
        ))
    ]
    for copy in local:
        copy.start()
    tiles[192] = jnp.zeros((128, 128), BF16)
    cell = lax.broadcasted_iota(jnp.int32, (8, 128), 0) * 128 + lax.broadcasted_iota(jnp.int32, (8, 128), 1)
    live = count[0, 0]

    def find(s, table):
        return jnp.where((cell == slots[0, s]) & (s < live), s, table)

    inv_v[...] = lax.fori_loop(0, 192, find, jnp.full((8, 128), 192, jnp.int32), unroll=8)
    place_table = pltpu.make_async_copy(inv_v, inv, tsem.at[4])
    place_table.start()
    local[0].wait()
    pl.semaphore_wait(barrier, 17)

    for i in (4, 1, 3, 2, 5, 7, 6):
        send(xpan.at[r], xpan.at[r], "feat", i, at_row(i))
    place_table.wait()
    local[1].wait()

    def pair(row, p):
        n, at = row // 8, (row % 8) * 16 + 2 * p
        return jnp.concatenate([tiles[inv[n, at]], tiles[inv[n, at + 1]]], axis=1)

    def product(zt, kt, blocks):
        total = None
        for p in blocks:
            rows = [pair(2 * ((q // 2) * 16 + zt * 2 + kt) + q % 2, p) for q in range(4)]
            part = jnp.dot(jnp.concatenate(rows, axis=0), xpan[p], preferred_element_type=F32)
            total = part if total is None else total + part
        return total

    @pl.loop(0, 16)
    def _(j):
        pacc[j // 2, j % 2] = product(j // 2, j % 2, [r])

    for i in (1, 3, 4):
        arrive(xpan.at[row_from(i)], "feat", i)

    @pl.loop(0, 16)
    def _(j):
        pacc[j // 2, j % 2] += product(j // 2, j % 2, [row_from(i) for i in (1, 3, 4)])

    for i in (2, 5, 7, 6):
        arrive(xpan.at[row_from(i)], "feat", i)

    def side(q):
        return xl if q else ox

    def forward(g, h):
        zt = (z + DIST[g] + 8) % 8
        kt = k if h else ok
        pacc[zt, kt] += product(zt, kt, [row_from(i) for i in (2, 5, 7, 6)])
        if h == 0:
            for q in range(2):
                ks[g, q] = pacc[zt, kt, pl.ds(q * N, N)].astype(BF16)
            send(ks.at[g], kr.at[g], "core", g, at_core())

    def chip_sum(g, q, first, last):
        zt, x = (z + DIST[g] + 8) % 8, side(q)
        return pacc[zt, k, pl.ds(x * N + first, last - first)] + kr[g, x, first:last].astype(F32)

    def way(d):
        return (0, 4 - d) if d > 0 else (1, 4 + d)

    def chip(g):
        arrive(kr.at[g], "core", g)
        sxs[g] = chip_sum(g, 0, 0, A).astype(BF16)
        send(sxs.at[g], rx.at[g], "xrow", g, at_x())
        sx[g] = chip_sum(g, 1, 0, A)

    def ring_z(g, q):
        s = chip_sum(g, q, A, N)
        w, step = (q, 0) if DIST[g] == 4 else way(DIST[g])
        if step > 1 or (step == 1 and q == w):
            arrive(rz.at[w, step - 1, q], "ringz", (w * 4 + step - 1) * 2 + q)
            s = s + rz[w, step - 1, q].astype(F32)
        zs[g, q] = s.astype(BF16)
        send(zs.at[g, q], rz.at[w, step, q], "ringz", (w * 4 + step) * 2 + q, at_z(1 - 2 * w))

    def ring_x(g):
        d = DIST[g]
        arrive(rx.at[g], "xrow", g)
        s = sx[g] + rx[g].astype(F32)
        if d == 4:
            qs[g] = s.astype(BF16)
            for w in range(2):
                rows = pl.ds(w * (A // 2), A // 2)
                send(qs.at[g, rows], rq.at[w, 0, rows], "ringx", w * 4, at_z(1 - 2 * w))
            return
        w, step = way(d)
        if step == 1:
            rows = pl.ds(w * (A // 2), A // 2)
            arrive(rq.at[w, 0, rows], "ringx", w * 4)
            sx[g] = s
            sx[g, rows] += rq[w, 0, rows].astype(F32)
            s = sx[g]
        else:
            arrive(rq.at[w, step - 1], "ringx", w * 4 + step - 1)
            s = s + rq[w, step - 1].astype(F32)
        qs[g] = s.astype(BF16)
        send(qs.at[g], rq.at[w, step], "ringx", w * 4 + step, at_z(1 - 2 * w))

    def last_z(q):
        for w in range(2):
            arrive(rz.at[w, 3, q], "ringz", (w * 4 + 3) * 2 + q)
        s = chip_sum(7, q, A, N) + rz[0, 3, q].astype(F32) + rz[1, 3, q].astype(F32)
        if q == 0:
            xfs[...] = s.astype(BF16)
            send(xfs, xfr, "xfin", 0, at_x())
        else:
            zf[...] = s

    for op in SUMS:
        if op[:2] == "Fa":
            forward(int(op[2]), 0)
        elif op[:2] == "Fb":
            forward(int(op[2]), 1)
        elif op[0] == "S":
            chip(int(op[1]))
        elif op[0] == "Z":
            ring_z(int(op[1]), int(op[2]))
        elif op[0] == "X":
            ring_x(int(op[1]))
        elif op in ("P0", "P1"):
            last_z(int(op[1]))
    arrive(rx.at[7], "xrow", 7)
    for w in range(2):
        arrive(rq.at[w, 3], "ringx", w * 4 + 3)
    head = (sx[7] + rx[7].astype(F32) + rq[0, 3].astype(F32) + rq[1, 3].astype(F32)).astype(BF16)
    arrive(xfr, "xfin", 0)
    tail = (zf[...] + xfr[...].astype(F32)).astype(BF16)
    local[2].wait()
    local[3].wait()

    hidden = jnp.concatenate([head, tail], axis=0)
    preact = jnp.dot(hidden, weight[...], preferred_element_type=F32)
    sig = jax.nn.sigmoid(preact)
    layer_out[...] = (preact * sig).astype(BF16)
    act = (cot[...].astype(F32) * sig * (1.0 + preact * (1.0 - sig))).astype(BF16)
    hp[z, k, xl] = jnp.dot(act, weight[...].T, preferred_element_type=F32).astype(BF16)

    head_rows, tail_rows = pl.ds(0, B), pl.ds(B, N - B)
    mine = hp.at[z, k, xl]
    mine_head, mine_tail = mine.at[head_rows], mine.at[tail_rows]
    send(mine_tail, mine_tail, "xv", 0, at_x())
    send(mine_head, mine_head, "head", 0, at_z(1))
    send(mine_head, mine_head, "head", 4, at_z(-1))
    send(mine_head, mine_head, "xu", 0, at_x())
    send(mine_tail, mine_tail, "tail", 0, at_z(1))
    send(mine_tail, mine_tail, "tail", 4, at_z(-1))

    def place(d):
        return (z + d + 8) % 8

    def came_from(w, step):
        return place(-1 - step) if w == 0 else place(1 + step)

    def number(d):
        return d if d >= 0 else 8 + d

    def head_step(w, step):
        dist = 4 if step == 3 else (1 + step if w else -1 - step)
        rows = hp.at[came_from(w, step), k, xl, head_rows]
        arrive(rows, "head", w * 4 + step)
        if step < 2 or (step == 2 and w == 0):
            send(rows, rows, "head", w * 4 + step + 1, at_z(1 - 2 * w))
        send(rows, rows, "xu", number(dist), at_x())

    def tail_step(w, step):
        rows = hp.at[came_from(w, step), k, xl, tail_rows]
        arrive(rows, "tail", w * 4 + step)
        if step < 2 or (step == 2 and w == 1):
            send(rows, rows, "tail", w * 4 + step + 1, at_z(1 - 2 * w))

    def part_step(w, step):
        to = at_z(1 - 2 * w)
        block = hp.at[came_from(w, step), k, ox]
        rows = block.at[tail_rows] if step < 3 else block.at[pl.ds(B + w * 64, 64)]
        arrive(rows, "part", w * 4 + step)
        if step < 2:
            send(rows, rows, "part", w * 4 + step + 1, to)
        elif step == 2:
            half = block.at[pl.ds(B + w * 64, 64)]
            send(half, half, "part", w * 4 + 3, to)

    def share(d):
        block = hp.at[place(d), k, ox, head_rows]
        arrive(block, "xu", number(d))
        both = hp.at[place(d), k]
        send(both, both, "pair", number(d), at_core())

    def have(d):
        arrive(hp.at[place(d), ok], "pair", number(d))
        lt[...] = jnp.concatenate([hp[place(d), q // 2, q % 2] for q in range(4)], axis=0).T

    def add_product(d, n):
        rows = [pair(2 * (((q // 2) % 2) * 16 + place(d) * 2 + q // 4) + q % 2, n) for q in range(8)]
        acc[n] += jnp.dot(lt[...], jnp.concatenate(rows, axis=0), preferred_element_type=F32)

    def backward(d, part):
        if part == 0:
            have(d)

        @pl.loop(2 * part, 2 * part + 2)
        def _(n):
            add_product(d, n)

    def x_tail():
        rows = hp.at[z, k, ox, tail_rows]
        arrive(rows, "xv", 0)
        send(rows, rows, "part", 0, at_z(1))
        send(rows, rows, "part", 4, at_z(-1))

    def gradient_step(step):
        if step == 1:
            w1s[...] = jnp.dot(hidden.T, act, preferred_element_type=F32).reshape(8, 32, N)
            for i in range(1, 8):
                send(w1s.at[row_of(i)], w1r.at[r], "w1", i, at_row(i))
            acc[...] = jnp.zeros_like(acc)
        elif step == 2:
            for i in range(1, 8):
                arrive(w1r.at[row_from(i)], "w1", i)
            w1r[r] = w1s[r]
            s = w1r[0]
            for i in range(1, 8):
                s = s + w1r[i]
            for i in range(8):
                w2s[i] = s[(i // 2) * 8:(i // 2) * 8 + 8, (i % 2) * 128:(i % 2) * 128 + 128]
            for i in range(1, 8):
                send(w2s.at[place(i)], w2r.at[z], "w2", i, at_z(i))
        elif step == 3:
            for i in range(1, 8):
                arrive(w2r.at[place(-i)], "w2", i)
            w2r[z] = w2s[z]
            s = w2r[0]
            for i in range(1, 8):
                s = s + w2r[i]
            w3r[xl * 2 + k] = s
            for i in range(1, 4):
                send(w3r.at[xl * 2 + k], w3r.at[xl * 2 + k], "w3", i, at_mate(i))
        elif step == 4:
            for i in range(1, 4):
                arrive(w3r.at[((xl + i // 2) % 2) * 2 + (k + i % 2) % 2], "w3", i)
            w4r[r] = (w3r[0] + w3r[1]) + (w3r[2] + w3r[3])
            for i in range(1, 8):
                send(w4r.at[r], w4r.at[r], "w4", i, at_row(i))
        else:
            for i in range(1, 8):
                arrive(w4r.at[row_from(i)], "w4", i)
            w5r[z] = w4r[...]
            for i in range(1, 8):
                send(w5r.at[z], w5r.at[z], "w5", i, at_z(i))

    for op in GATHER:
        if op[:2] == "OH":
            head_step(int(op[2]), int(op[3]))
        elif op[:2] == "OT":
            tail_step(int(op[2]), int(op[3]))
        elif op[:2] == "PT":
            part_step(int(op[2]), int(op[3]))
        elif op[:2] == "SH":
            share(int(op[2:]))
        elif op[0] == "C":
            d, part = op[1:].split(",")
            backward(int(d), int(part))
        elif op[0] == "W":
            gradient_step(int(op[1]))
        else:
            x_tail()

    have(4)

    @pl.loop(0, 8)
    def _(j):
        i = (j + 1) % 8
        n = row_of(i)
        add_product(4, n)

        @pl.when(i != 0)
        def _():
            gs[n] = acc[n].astype(BF16)
            desc(gs.at[n], gr.at[r], "grad", i, at_row(i)).start()

    gradient_step(5)
    s = acc[r]
    for i in range(1, 8):
        arrive(gr.at[row_from(i)], "grad", i)
        s = s + gr[row_from(i)].astype(F32)
    feature_grad[...] = s.T.astype(BF16)
    for i in range(1, 8):
        arrive(w5r.at[place(-i)], "w5", i)
    for i in range(8):
        for j in range(8):
            first = j * 32 + (i // 2) * 8
            weight_grad[first:first + 8, (i % 2) * 128:(i % 2) * 128 + 128] = w5r[i, j] * (65536.0 ** -0.5)
    for d in sent:
        d.wait_send()
    for i in range(1, 8):
        desc(gs.at[row_of(i)], gr.at[r], "grad", i, at_row(i)).wait_send()


def hand_over(a, b, c, a_out, b_out, c_out):
    a_out[...] = a[...]
    b_out[...] = b[...]
    c_out[...] = c[...]


def body(features, edge_tiles, tile_slot, tile_count, weight, cotangent):
    vmem = pl.BlockSpec(memory_space=pltpu.VMEM)

    def buf(*shape, dtype=BF16):
        return pltpu.VMEM(shape, dtype)

    hbm = pl.BlockSpec(memory_space=pl.ANY)
    smem = pl.BlockSpec(memory_space=pltpu.SMEM)
    shapes = (
        jax.ShapeDtypeStruct((N, N), BF16),
        jax.ShapeDtypeStruct((N, N), F32),
        jax.ShapeDtypeStruct((N, N), BF16),
    )
    results = pl.pallas_call(
        kernel,
        out_shape=shapes,
        in_specs=[smem, smem, hbm, hbm, hbm, hbm],
        out_specs=(vmem, vmem, vmem),
        scratch_shapes=[
            buf(193, 128, 128),
            buf(8, N, N),
            buf(8, 2, 2 * N, N, dtype=F32),
            buf(8, 2, N, N),
            buf(8, 2, N, N),
            buf(8, A, N),
            buf(8, A, N, dtype=F32),
            buf(8, A, N),
            buf(7, 2, N - A, N),
            buf(2, 4, 2, N - A, N),
            buf(7, A, N),
            buf(2, 4, A, N),
            buf(N - A, N),
            buf(N - A, N),
            buf(N - A, N, dtype=F32),
            buf(8, 2, 2, N, N),
            buf(N, 4 * N),
            buf(8, N, N, dtype=F32),
            buf(8, 32, N, dtype=F32),
            buf(8, 32, N, dtype=F32),
            buf(8, 8, 128, dtype=F32),
            buf(8, 8, 128, dtype=F32),
            buf(4, 8, 128, dtype=F32),
            buf(8, 8, 128, dtype=F32),
            buf(8, 8, 8, 128, dtype=F32),
            buf(8, N, N),
            buf(8, N, N),
            buf(N, N),
            buf(N, N),
            buf(8, 128, dtype=jnp.int32),
            pltpu.SMEM((8, 128), jnp.int32),
            pltpu.SemaphoreType.DMA((TOTAL,)),
            pltpu.SemaphoreType.DMA((TOTAL,)),
            pltpu.SemaphoreType.DMA((5,)),
        ],
        compiler_params=pltpu.CompilerParams(
            collective_id=0, has_side_effects=True, vmem_limit_bytes=56 * 2**20
        ),
    )(tile_slot, tile_count, features, edge_tiles.reshape(192, 128, 128), weight, cotangent)
    return pl.pallas_call(
        hand_over,
        out_shape=shapes,
        in_specs=[vmem] * 3,
        out_specs=(vmem,) * 3,
    )(*results)


def solution(mesh):
    in_specs = (
        P(("col", "row"), None),
        P("row", "col", None, None),
        P("row", "col"),
        P("row", "col"),
        P(),
        P(("row", "col"), None),
    )
    out_specs = (P(("row", "col"), None), P(), P(("col", "row"), None))
    return jax.shard_map(body, mesh=mesh, in_specs=in_specs, out_specs=out_specs, check_vma=False)
```

```python
import functools

import jax
import jax.numpy as jnp
from jax import lax
from jax.experimental import pallas as pl
from jax.experimental.pallas import tpu as pltpu
from jax.sharding import PartitionSpec as P

F32 = jnp.float32
BF16 = jnp.bfloat16
MESH = pl.DeviceIdType.MESH
N = 256
A = 128
B = 128
DIST = (4, 3, -3, 2, -2, 1, -1, 0)
SEMS = dict(
    feat=8, core=8, xrow=8, ringz=16, ringx=8, xfin=1,
    head=8, tail=8, part=8, xv=1, xu=8, pair=8,
    w1=8, w2=8, w3=4, w4=8, w5=8, grad=8,
)
SUMS = (
    "Fa0", "Fb0", "Fa1", "Fb1", "S0", "Z00", "Z01", "Fa2", "S1", "Z11", "Fb2", "Fa3", "S2", "Z20", "Fb3", "X0", "Z10",
    "Z21", "S3", "Fa4", "Fb4", "Z31", "Fa5", "S4", "Z40", "X1", "Fb5", "X2", "S5", "Z30", "Fa6", "Z41", "Fb6", "Z51",
    "Fa7", "S6", "Z60", "X3", "Fb7", "X4", "S7", "Z50", "Z61", "X5", "X6", "P0", "P1", "P2", "P3",
)
GATHER = (
    "B0", "OH00", "OH10", "V", "W1", "OT10", "OT00", "SH0", "B1", "B-1", "C0,0", "C0,1", "OH01", "OH11", "C0,2",
    "C0,3", "PT00", "SH-1", "PT10", "SH1", "OT01", "OT11", "C-1,0", "C-1,1", "C-1,2", "C-1,3", "OH12", "OH02", "C1,0",
    "C1,1", "W2", "PT01", "PT11", "SH-2", "C1,2", "C1,3", "SH2", "OT02", "OT12", "C-2,0", "C-2,1", "OH03", "C-2,2",
    "C-2,3", "C2,0", "PT02", "SH-3", "PT12", "SH3", "C2,1", "C2,2", "OT13", "C2,3", "C-3,0", "C-3,1", "C-3,2", "PT13",
    "PT03", "SH4", "C-3,3", "C3,0", "C3,1", "W3", "C3,2", "C3,3", "W4",
)
OFFSET = {}
TOTAL = 0
for _name, _count in SEMS.items():
    OFFSET[_name] = TOTAL
    TOTAL += _count


def kernel(
    slots, count, feat, tiles_hbm, weight_hbm, cot_hbm,
    layer_out, weight_grad, feature_grad,
    tiles, xpan, pacc, ks, kr, sxs, sx, rx, zs, rz, qs, rq, xfs, xfr, zf,
    hp, acc, w1s, w1r, w2s, w2r, w3r, w4r, w5r, gs, gr, weight, cot, inv_v, inv,
    ssem, rsem, tsem,
):
    r = lax.axis_index("row")
    c = lax.axis_index("col")
    xh, y = r // 4, r % 4
    xl, z, k = c // 16, (c % 16) // 2, c % 2
    ox, ok = 1 - xl, 1 - k

    def row_of(i):
        return ((xh + i // 4) % 2) * 4 + (y + i % 4) % 4

    def row_from(i):
        return ((xh + i // 4) % 2) * 4 + (y + 4 - i % 4) % 4

    def at_row(i):
        return (row_of(i), c)

    def at_z(d):
        return (r, xl * 16 + ((z + d + 8) % 8) * 2 + k)

    def at_x():
        return (r, ox * 16 + z * 2 + k)

    def at_core():
        return (r, xl * 16 + z * 2 + ok)

    def at_mate(i):
        return (r, ((xl + i // 2) % 2) * 16 + z * 2 + (k + i % 2) % 2)

    sent = []

    def desc(src, dst, name, i, to):
        return pltpu.make_async_remote_copy(
            src_ref=src, dst_ref=dst, send_sem=ssem.at[OFFSET[name] + i],
            recv_sem=rsem.at[OFFSET[name] + i], device_id=to, device_id_type=MESH,
        )

    def send(src, dst, name, i, to):
        d = desc(src, dst, name, i, to)
        d.start()
        sent.append(d)

    def arrive(dst, name, i):
        desc(dst, dst, name, i, at_core()).wait_recv()

    barrier = pltpu.get_barrier_semaphore()
    for i in range(1, 8):
        pl.semaphore_signal(barrier, inc=1, device_id=at_row(i), device_id_type=MESH)
        pl.semaphore_signal(barrier, inc=1, device_id=at_z(i), device_id_type=MESH)
    for i in range(1, 4):
        pl.semaphore_signal(barrier, inc=1, device_id=at_mate(i), device_id_type=MESH)
    local = [
        pltpu.make_async_copy(src, dst, tsem.at[i])
        for i, (src, dst) in enumerate((
            (feat, xpan.at[r]), (tiles_hbm, tiles.at[pl.ds(0, 192)]), (weight_hbm, weight), (cot_hbm, cot),
        ))
    ]
    for copy in local:
        copy.start()
    tiles[192] = jnp.zeros((128, 128), BF16)
    cell = lax.broadcasted_iota(jnp.int32, (8, 128), 0) * 128 + lax.broadcasted_iota(jnp.int32, (8, 128), 1)
    live = count[0, 0]

    def find(s, table):
        return jnp.where((cell == slots[0, s]) & (s < live), s, table)

    inv_v[...] = lax.fori_loop(0, 192, find, jnp.full((8, 128), 192, jnp.int32), unroll=8)
    place_table = pltpu.make_async_copy(inv_v, inv, tsem.at[4])
    place_table.start()
    local[0].wait()
    pl.semaphore_wait(barrier, 17)

    for i in (4, 1, 3, 2, 5, 7, 6):
        send(xpan.at[r], xpan.at[r], "feat", i, at_row(i))
    place_table.wait()
    local[1].wait()

    def pair(row, p):
        n, at = row // 8, (row % 8) * 16 + 2 * p
        return jnp.concatenate([tiles[inv[n, at]], tiles[inv[n, at + 1]]], axis=1)

    def product(zt, kt, blocks):
        total = None
        for p in blocks:
            rows = [pair(2 * ((q // 2) * 16 + zt * 2 + kt) + q % 2, p) for q in range(4)]
            part = jnp.dot(jnp.concatenate(rows, axis=0), xpan[p], preferred_element_type=F32)
            total = part if total is None else total + part
        return total

    @pl.loop(0, 16)
    def _(j):
        pacc[j // 2, j % 2] = product(j // 2, j % 2, [r])

    for i in (1, 3, 4):
        arrive(xpan.at[row_from(i)], "feat", i)

    @pl.loop(0, 16)
    def _(j):
        pacc[j // 2, j % 2] += product(j // 2, j % 2, [row_from(i) for i in (1, 3, 4)])

    for i in (2, 5, 7, 6):
        arrive(xpan.at[row_from(i)], "feat", i)

    def side(q):
        return xl if q else ox

    def forward(g, h):
        zt = (z + DIST[g] + 8) % 8
        kt = k if h else ok
        pacc[zt, kt] += product(zt, kt, [row_from(i) for i in (2, 5, 7, 6)])
        if h == 0:
            for q in range(2):
                ks[g, q] = pacc[zt, kt, pl.ds(q * N, N)].astype(BF16)
            send(ks.at[g], kr.at[g], "core", g, at_core())

    def chip_sum(g, q, first, last):
        zt, x = (z + DIST[g] + 8) % 8, side(q)
        return pacc[zt, k, pl.ds(x * N + first, last - first)] + kr[g, x, first:last].astype(F32)

    def way(d):
        return (0, 4 - d) if d > 0 else (1, 4 + d)

    def chip(g):
        arrive(kr.at[g], "core", g)
        sxs[g] = chip_sum(g, 0, 0, A).astype(BF16)
        send(sxs.at[g], rx.at[g], "xrow", g, at_x())
        sx[g] = chip_sum(g, 1, 0, A)

    def ring_z(g, q):
        s = chip_sum(g, q, A, N)
        w, step = (q, 0) if DIST[g] == 4 else way(DIST[g])
        if step > 1 or (step == 1 and q == w):
            arrive(rz.at[w, step - 1, q], "ringz", (w * 4 + step - 1) * 2 + q)
            s = s + rz[w, step - 1, q].astype(F32)
        zs[g, q] = s.astype(BF16)
        send(zs.at[g, q], rz.at[w, step, q], "ringz", (w * 4 + step) * 2 + q, at_z(1 - 2 * w))

    def ring_x(g):
        d = DIST[g]
        arrive(rx.at[g], "xrow", g)
        s = sx[g] + rx[g].astype(F32)
        if d == 4:
            qs[g] = s.astype(BF16)
            for w in range(2):
                rows = pl.ds(w * (A // 2), A // 2)
                send(qs.at[g, rows], rq.at[w, 0, rows], "ringx", w * 4, at_z(1 - 2 * w))
            return
        w, step = way(d)
        if step == 1:
            rows = pl.ds(w * (A // 2), A // 2)
            arrive(rq.at[w, 0, rows], "ringx", w * 4)
            sx[g] = s
            sx[g, rows] += rq[w, 0, rows].astype(F32)
            s = sx[g]
        else:
            arrive(rq.at[w, step - 1], "ringx", w * 4 + step - 1)
            s = s + rq[w, step - 1].astype(F32)
        qs[g] = s.astype(BF16)
        send(qs.at[g], rq.at[w, step], "ringx", w * 4 + step, at_z(1 - 2 * w))

    def last_z(q):
        for w in range(2):
            arrive(rz.at[w, 3, q], "ringz", (w * 4 + 3) * 2 + q)
        s = chip_sum(7, q, A, N) + rz[0, 3, q].astype(F32) + rz[1, 3, q].astype(F32)
        if q == 0:
            xfs[...] = s.astype(BF16)
            send(xfs, xfr, "xfin", 0, at_x())
        else:
            zf[...] = s

    for op in SUMS:
        if op[:2] == "Fa":
            forward(int(op[2]), 0)
        elif op[:2] == "Fb":
            forward(int(op[2]), 1)
        elif op[0] == "S":
            chip(int(op[1]))
        elif op[0] == "Z":
            ring_z(int(op[1]), int(op[2]))
        elif op[0] == "X":
            ring_x(int(op[1]))
        elif op in ("P0", "P1"):
            last_z(int(op[1]))
    arrive(rx.at[7], "xrow", 7)
    for w in range(2):
        arrive(rq.at[w, 3], "ringx", w * 4 + 3)
    head = (sx[7] + rx[7].astype(F32) + rq[0, 3].astype(F32) + rq[1, 3].astype(F32)).astype(BF16)
    arrive(xfr, "xfin", 0)
    tail = (zf[...] + xfr[...].astype(F32)).astype(BF16)
    local[2].wait()
    local[3].wait()

    hidden = jnp.concatenate([head, tail], axis=0)
    preact = jnp.dot(hidden, weight[...], preferred_element_type=F32)
    sig = jax.nn.sigmoid(preact)
    layer_out[...] = (preact * sig).astype(BF16)
    act = (cot[...].astype(F32) * sig * (1.0 + preact * (1.0 - sig))).astype(BF16)
    hp[z, k, xl] = jnp.dot(weight[...], act.T, preferred_element_type=F32).astype(BF16)

    head_rows, tail_rows = pl.ds(0, B), pl.ds(B, N - B)
    mine = hp.at[z, k, xl]
    mine_head, mine_tail = mine.at[head_rows], mine.at[tail_rows]
    send(mine_tail, mine_tail, "xv", 0, at_x())
    send(mine_head, mine_head, "head", 0, at_z(1))
    send(mine_head, mine_head, "head", 4, at_z(-1))
    send(mine_head, mine_head, "xu", 0, at_x())
    send(mine_tail, mine_tail, "tail", 0, at_z(1))
    send(mine_tail, mine_tail, "tail", 4, at_z(-1))

    def place(d):
        return (z + d + 8) % 8

    def came_from(w, step):
        return place(-1 - step) if w == 0 else place(1 + step)

    def number(d):
        return d if d >= 0 else 8 + d

    def head_step(w, step):
        dist = 4 if step == 3 else (1 + step if w else -1 - step)
        rows = hp.at[came_from(w, step), k, xl, head_rows]
        arrive(rows, "head", w * 4 + step)
        if step < 2 or (step == 2 and w == 0):
            send(rows, rows, "head", w * 4 + step + 1, at_z(1 - 2 * w))
        send(rows, rows, "xu", number(dist), at_x())

    def tail_step(w, step):
        rows = hp.at[came_from(w, step), k, xl, tail_rows]
        arrive(rows, "tail", w * 4 + step)
        if step < 2 or (step == 2 and w == 1):
            send(rows, rows, "tail", w * 4 + step + 1, at_z(1 - 2 * w))

    def part_step(w, step):
        to = at_z(1 - 2 * w)
        block = hp.at[came_from(w, step), k, ox]
        rows = block.at[tail_rows] if step < 3 else block.at[pl.ds(B + w * 64, 64)]
        arrive(rows, "part", w * 4 + step)
        if step < 2:
            send(rows, rows, "part", w * 4 + step + 1, to)
        elif step == 2:
            half = block.at[pl.ds(B + w * 64, 64)]
            send(half, half, "part", w * 4 + 3, to)

    def share(d):
        block = hp.at[place(d), k, ox, head_rows]
        arrive(block, "xu", number(d))
        both = hp.at[place(d), k]
        send(both, both, "pair", number(d), at_core())

    def have(d):
        arrive(hp.at[place(d), ok], "pair", number(d))

    def add_product(d, n, own=None):
        blocks = [(k, xl), (k, ox), (ok, xl), (ok, ox)] if abs(d) < 2 else [(q // 2, q % 2) for q in range(4)]
        blocks = blocks if own is None else blocks[:1] if own else blocks[1:]
        left = jnp.concatenate([hp[place(d), u, v] for u, v in blocks], axis=1)
        rows = [pair(2 * (v * 16 + place(d) * 2 + u) + q, n) for u, v in blocks for q in range(2)]
        total = jnp.dot(left, jnp.concatenate(rows, axis=0), preferred_element_type=F32)
        if own and d == 0:
            acc[n] = total
        else:
            acc[n] += total

    def own_block(d):
        @pl.loop(0, 8)
        def _(n):
            add_product(d, n, True)

    def backward(d, part):
        if part == 0:
            have(d)

        @pl.loop(2 * part, 2 * part + 2)
        def _(n):
            add_product(d, n, False if abs(d) < 2 else None)

    def x_tail():
        rows = hp.at[z, k, ox, tail_rows]
        arrive(rows, "xv", 0)
        send(rows, rows, "part", 0, at_z(1))
        send(rows, rows, "part", 4, at_z(-1))

    def gradient_step(step):
        if step == 1:
            w1s[...] = jnp.dot(hidden.T, act, preferred_element_type=F32).reshape(8, 32, N)
            for i in range(1, 8):
                send(w1s.at[row_of(i)], w1r.at[r], "w1", i, at_row(i))
        elif step == 2:
            for i in range(1, 8):
                arrive(w1r.at[row_from(i)], "w1", i)
            w1r[r] = w1s[r]
            s = w1r[0]
            for i in range(1, 8):
                s = s + w1r[i]
            for i in range(8):
                w2s[i] = s[(i // 2) * 8:(i // 2) * 8 + 8, (i % 2) * 128:(i % 2) * 128 + 128]
            for i in range(1, 8):
                send(w2s.at[place(i)], w2r.at[z], "w2", i, at_z(i))
        elif step == 3:
            for i in range(1, 8):
                arrive(w2r.at[place(-i)], "w2", i)
            w2r[z] = w2s[z]
            s = w2r[0]
            for i in range(1, 8):
                s = s + w2r[i]
            w3r[xl * 2 + k] = s
            for i in range(1, 4):
                send(w3r.at[xl * 2 + k], w3r.at[xl * 2 + k], "w3", i, at_mate(i))
        elif step == 4:
            for i in range(1, 4):
                arrive(w3r.at[((xl + i // 2) % 2) * 2 + (k + i % 2) % 2], "w3", i)
            w4r[r] = (w3r[0] + w3r[1]) + (w3r[2] + w3r[3])
            for i in range(1, 8):
                send(w4r.at[r], w4r.at[r], "w4", i, at_row(i))
        else:
            for i in range(1, 8):
                arrive(w4r.at[row_from(i)], "w4", i)
            w5r[z] = w4r[...]
            for i in range(1, 8):
                send(w5r.at[z], w5r.at[z], "w5", i, at_z(i))

    for op in GATHER:
        if op[:2] == "OH":
            head_step(int(op[2]), int(op[3]))
        elif op[:2] == "OT":
            tail_step(int(op[2]), int(op[3]))
        elif op[:2] == "PT":
            part_step(int(op[2]), int(op[3]))
        elif op[:2] == "SH":
            share(int(op[2:]))
        elif op[0] == "B":
            own_block(int(op[1:]))
        elif op[0] == "C":
            d, part = op[1:].split(",")
            backward(int(d), int(part))
        elif op[0] == "W":
            gradient_step(int(op[1]))
        else:
            x_tail()

    have(4)

    @pl.loop(0, 8)
    def _(j):
        i = (j + 1) % 8
        n = row_of(i)
        add_product(4, n)

        @pl.when(i != 0)
        def _():
            gs[n] = acc[n].astype(BF16)
            desc(gs.at[n], gr.at[r], "grad", i, at_row(i)).start()

    gradient_step(5)
    s = acc[r]
    for i in range(1, 8):
        arrive(gr.at[row_from(i)], "grad", i)
        s = s + gr[row_from(i)].astype(F32)
    feature_grad[...] = s.T.astype(BF16)
    for i in range(1, 8):
        arrive(w5r.at[place(-i)], "w5", i)
    for i in range(8):
        for j in range(8):
            first = j * 32 + (i // 2) * 8
            weight_grad[first:first + 8, (i % 2) * 128:(i % 2) * 128 + 128] = w5r[i, j] * (65536.0 ** -0.5)
    for d in sent:
        d.wait_send()
    for i in range(1, 8):
        desc(gs.at[row_of(i)], gr.at[r], "grad", i, at_row(i)).wait_send()


def hand_over(a, b, c, a_out, b_out, c_out):
    a_out[...] = a[...]
    b_out[...] = b[...]
    c_out[...] = c[...]


def body(features, edge_tiles, tile_slot, tile_count, weight, cotangent):
    vmem = pl.BlockSpec(memory_space=pltpu.VMEM)

    def buf(*shape, dtype=BF16):
        return pltpu.VMEM(shape, dtype)

    hbm = pl.BlockSpec(memory_space=pl.ANY)
    smem = pl.BlockSpec(memory_space=pltpu.SMEM)
    shapes = (
        jax.ShapeDtypeStruct((N, N), BF16),
        jax.ShapeDtypeStruct((N, N), F32),
        jax.ShapeDtypeStruct((N, N), BF16),
    )
    results = pl.pallas_call(
        kernel,
        out_shape=shapes,
        in_specs=[smem, smem, hbm, hbm, hbm, hbm],
        out_specs=(vmem, vmem, vmem),
        scratch_shapes=[
            buf(193, 128, 128),
            buf(8, N, N),
            buf(8, 2, 2 * N, N, dtype=F32),
            buf(8, 2, N, N),
            buf(8, 2, N, N),
            buf(8, A, N),
            buf(8, A, N, dtype=F32),
            buf(8, A, N),
            buf(7, 2, N - A, N),
            buf(2, 4, 2, N - A, N),
            buf(7, A, N),
            buf(2, 4, A, N),
            buf(N - A, N),
            buf(N - A, N),
            buf(N - A, N, dtype=F32),
            buf(8, 2, 2, N, N),
            buf(8, N, N, dtype=F32),
            buf(8, 32, N, dtype=F32),
            buf(8, 32, N, dtype=F32),
            buf(8, 8, 128, dtype=F32),
            buf(8, 8, 128, dtype=F32),
            buf(4, 8, 128, dtype=F32),
            buf(8, 8, 128, dtype=F32),
            buf(8, 8, 8, 128, dtype=F32),
            buf(8, N, N),
            buf(8, N, N),
            buf(N, N),
            buf(N, N),
            buf(8, 128, dtype=jnp.int32),
            pltpu.SMEM((8, 128), jnp.int32),
            pltpu.SemaphoreType.DMA((TOTAL,)),
            pltpu.SemaphoreType.DMA((TOTAL,)),
            pltpu.SemaphoreType.DMA((5,)),
        ],
        compiler_params=pltpu.CompilerParams(
            collective_id=0, has_side_effects=True, vmem_limit_bytes=56 * 2**20
        ),
    )(tile_slot, tile_count, features, edge_tiles.reshape(192, 128, 128), weight, cotangent)
    return pl.pallas_call(
        hand_over,
        out_shape=shapes,
        in_specs=[vmem] * 3,
        out_specs=(vmem,) * 3,
    )(*results)


def solution(mesh):
    in_specs = (
        P(("col", "row"), None),
        P("row", "col", None, None),
        P("row", "col"),
        P("row", "col"),
        P(),
        P(("row", "col"), None),
    )
    out_specs = (P(("row", "col"), None), P(), P(("col", "row"), None))
    return jax.shard_map(body, mesh=mesh, in_specs=in_specs, out_specs=out_specs, check_vma=False)
```

```python
import functools

import jax
import jax.numpy as jnp
from jax import lax
from jax.experimental import pallas as pl
from jax.experimental.pallas import tpu as pltpu
from jax.sharding import PartitionSpec as P

F32 = jnp.float32
BF16 = jnp.bfloat16
MESH = pl.DeviceIdType.MESH
N = 256
A = 128
B = 128
DIST = (4, 3, -3, 2, -2, 1, -1, 0)
SEMS = dict(
    feat=8, core=8, xrow=8, ringz=16, ringx=8, xfin=1,
    head=8, tail=8, part=8, xv=1, xu=8, pair=8,
    w1=8, w2=8, w3=4, w4=8, w5=8, grad=8,
)
SUMS = (
    "Fa0", "Fb0", "Fa1", "Fb1", "S0", "Z00", "Z01", "Fa2", "S1", "Z11", "Fb2", "Fa3", "S2", "Z20", "Fb3", "X0", "Z10",
    "Z21", "S3", "Fa4", "Fb4", "Z31", "Fa5", "S4", "Z40", "X1", "Fb5", "X2", "S5", "Z30", "Fa6", "Z41", "Fb6", "Z51",
    "Fa7", "S6", "Z60", "X3", "Fb7", "X4", "S7", "Z50", "Z61", "X5", "X6", "P0", "P1", "P2", "P3",
)
GATHER = (
    "B0", "OH00", "OH10", "V", "W1", "OT10", "OT00", "SH0", "B1", "B-1", "C0,0", "C0,1", "OH01", "OH11", "C0,2",
    "C0,3", "PT00", "SH-1", "PT10", "SH1", "OT01", "OT11", "C-1,0", "C-1,1", "W2", "C-1,2", "C-1,3", "OH12", "OH02",
    "C1,0", "C1,1", "PT01", "PT11", "SH-2", "C1,2", "C1,3", "SH2", "OT02", "OT12", "C-2,0", "C-2,1", "OH03", "C-2,2",
    "C-2,3", "C2,0", "PT02", "SH-3", "PT12", "SH3", "C2,1", "C2,2", "OT13", "C2,3", "W3", "C-3,0", "C-3,1", "C-3,2",
    "PT13", "PT03", "SH4", "C-3,3", "W4", "C3,0", "C3,1", "C3,2", "C3,3",
)
OFFSET = {}
TOTAL = 0
for _name, _count in SEMS.items():
    OFFSET[_name] = TOTAL
    TOTAL += _count


def kernel(
    slots, count, feat, tiles_hbm, weight_hbm, cot_hbm,
    layer_out, weight_grad, feature_grad,
    tiles, xpan, pacc, ks, kr, sxs, sx, rx, zs, rz, qs, rq, xfs, xfr, zf,
    hp, acc, w1s, w1r, w2s, w2r, w3r, w4r, w5r, gs, gr, weight, cot, inv_v, inv,
    ssem, rsem, tsem,
):
    r = lax.axis_index("row")
    c = lax.axis_index("col")
    xh, y = r // 4, r % 4
    xl, z, k = c // 16, (c % 16) // 2, c % 2
    ox, ok = 1 - xl, 1 - k

    def row_of(i):
        return ((xh + i // 4) % 2) * 4 + (y + i % 4) % 4

    def row_from(i):
        return ((xh + i // 4) % 2) * 4 + (y + 4 - i % 4) % 4

    def at_row(i):
        return (row_of(i), c)

    def at_z(d):
        return (r, xl * 16 + ((z + d + 8) % 8) * 2 + k)

    def at_x():
        return (r, ox * 16 + z * 2 + k)

    def at_core():
        return (r, xl * 16 + z * 2 + ok)

    def at_mate(i):
        return (r, ((xl + i // 2) % 2) * 16 + z * 2 + (k + i % 2) % 2)

    sent = []

    def desc(src, dst, name, i, to):
        return pltpu.make_async_remote_copy(
            src_ref=src, dst_ref=dst, send_sem=ssem.at[OFFSET[name] + i],
            recv_sem=rsem.at[OFFSET[name] + i], device_id=to, device_id_type=MESH,
        )

    def send(src, dst, name, i, to):
        d = desc(src, dst, name, i, to)
        d.start()
        sent.append(d)

    def arrive(dst, name, i):
        desc(dst, dst, name, i, at_core()).wait_recv()

    barrier = pltpu.get_barrier_semaphore()
    for i in range(1, 8):
        pl.semaphore_signal(barrier, inc=1, device_id=at_row(i), device_id_type=MESH)
        pl.semaphore_signal(barrier, inc=1, device_id=at_z(i), device_id_type=MESH)
    for i in range(1, 4):
        pl.semaphore_signal(barrier, inc=1, device_id=at_mate(i), device_id_type=MESH)
    local = [
        pltpu.make_async_copy(src, dst, tsem.at[i])
        for i, (src, dst) in enumerate((
            (feat, xpan.at[r]), (tiles_hbm, tiles.at[pl.ds(0, 192)]), (weight_hbm, weight), (cot_hbm, cot),
        ))
    ]
    for copy in local:
        copy.start()
    tiles[192] = jnp.zeros((128, 128), BF16)
    cell = lax.broadcasted_iota(jnp.int32, (8, 128), 0) * 128 + lax.broadcasted_iota(jnp.int32, (8, 128), 1)
    live = count[0, 0]

    def find(s, table):
        return jnp.where((cell == slots[0, s]) & (s < live), s, table)

    inv_v[...] = lax.fori_loop(0, 192, find, jnp.full((8, 128), 192, jnp.int32), unroll=8)
    place_table = pltpu.make_async_copy(inv_v, inv, tsem.at[4])
    place_table.start()
    local[0].wait()
    pl.semaphore_wait(barrier, 17)

    for i in (4, 1, 3, 2, 5, 7, 6):
        send(xpan.at[r], xpan.at[r], "feat", i, at_row(i))
    place_table.wait()
    local[1].wait()

    two = jnp.int32(2)

    def spot(zt):
        return zt, lax.div(zt, two), lax.rem(zt, two) * 64

    def pair(n, at):
        return jnp.concatenate([tiles[inv[n, at]], tiles[inv[n, at + 1]]], axis=1)

    def product(where, kt, blocks):
        _, half, begin = where
        begin = begin + kt * 32
        total = None
        for p in blocks:
            at = begin + 2 * p
            rows = [pair(half + (q // 2) * 4, at + (q % 2) * 16) for q in range(4)]
            part = jnp.dot(jnp.concatenate(rows, axis=0), xpan[p], preferred_element_type=F32)
            total = part if total is None else total + part
        return total

    @pl.loop(0, 16)
    def _(j):
        zt, kt = lax.div(j, two), lax.rem(j, two)
        pacc[zt, kt] = product(spot(zt), kt, [r])

    for i in (1, 3, 4):
        arrive(xpan.at[row_from(i)], "feat", i)
    early = [row_from(i) for i in (1, 3, 4)]
    late = [row_from(i) for i in (2, 5, 7, 6)]

    @pl.loop(0, 16)
    def _(j):
        zt, kt = lax.div(j, two), lax.rem(j, two)
        pacc[zt, kt] += product(spot(zt), kt, early)

    for i in (2, 5, 7, 6):
        arrive(xpan.at[row_from(i)], "feat", i)

    def side(q):
        return xl if q else ox

    def forward(g, h):
        zt = (z + DIST[g] + 8) % 8
        kt = k if h else ok
        pacc[zt, kt] += product(spot(zt), kt, late)
        if h == 0:
            for q in range(2):
                ks[g, q] = pacc[zt, kt, pl.ds(q * N, N)].astype(BF16)
            send(ks.at[g], kr.at[g], "core", g, at_core())

    def chip_sum(g, q, first, last):
        zt, x = (z + DIST[g] + 8) % 8, side(q)
        return pacc[zt, k, pl.ds(x * N + first, last - first)] + kr[g, x, first:last].astype(F32)

    def way(d):
        return (0, 4 - d) if d > 0 else (1, 4 + d)

    def chip(g):
        arrive(kr.at[g], "core", g)
        sxs[g] = chip_sum(g, 0, 0, A).astype(BF16)
        send(sxs.at[g], rx.at[g], "xrow", g, at_x())
        sx[g] = chip_sum(g, 1, 0, A)

    def ring_z(g, q):
        s = chip_sum(g, q, A, N)
        w, step = (q, 0) if DIST[g] == 4 else way(DIST[g])
        if step > 1 or (step == 1 and q == w):
            arrive(rz.at[w, step - 1, q], "ringz", (w * 4 + step - 1) * 2 + q)
            s = s + rz[w, step - 1, q].astype(F32)
        zs[g, q] = s.astype(BF16)
        send(zs.at[g, q], rz.at[w, step, q], "ringz", (w * 4 + step) * 2 + q, at_z(1 - 2 * w))

    def ring_x(g):
        d = DIST[g]
        arrive(rx.at[g], "xrow", g)
        s = sx[g] + rx[g].astype(F32)
        if d == 4:
            qs[g] = s.astype(BF16)
            for w in range(2):
                rows = pl.ds(w * (A // 2), A // 2)
                send(qs.at[g, rows], rq.at[w, 0, rows], "ringx", w * 4, at_z(1 - 2 * w))
            return
        w, step = way(d)
        if step == 1:
            rows = pl.ds(w * (A // 2), A // 2)
            arrive(rq.at[w, 0, rows], "ringx", w * 4)
            sx[g] = s
            sx[g, rows] += rq[w, 0, rows].astype(F32)
            s = sx[g]
        else:
            arrive(rq.at[w, step - 1], "ringx", w * 4 + step - 1)
            s = s + rq[w, step - 1].astype(F32)
        qs[g] = s.astype(BF16)
        send(qs.at[g], rq.at[w, step], "ringx", w * 4 + step, at_z(1 - 2 * w))

    def last_z(q):
        for w in range(2):
            arrive(rz.at[w, 3, q], "ringz", (w * 4 + 3) * 2 + q)
        s = chip_sum(7, q, A, N) + rz[0, 3, q].astype(F32) + rz[1, 3, q].astype(F32)
        if q == 0:
            xfs[...] = s.astype(BF16)
            send(xfs, xfr, "xfin", 0, at_x())
        else:
            zf[...] = s

    for op in SUMS:
        if op[:2] == "Fa":
            forward(int(op[2]), 0)
        elif op[:2] == "Fb":
            forward(int(op[2]), 1)
        elif op[0] == "S":
            chip(int(op[1]))
        elif op[0] == "Z":
            ring_z(int(op[1]), int(op[2]))
        elif op[0] == "X":
            ring_x(int(op[1]))
        elif op in ("P0", "P1"):
            last_z(int(op[1]))
    arrive(rx.at[7], "xrow", 7)
    for w in range(2):
        arrive(rq.at[w, 3], "ringx", w * 4 + 3)
    head = (sx[7] + rx[7].astype(F32) + rq[0, 3].astype(F32) + rq[1, 3].astype(F32)).astype(BF16)
    arrive(xfr, "xfin", 0)
    tail = (zf[...] + xfr[...].astype(F32)).astype(BF16)
    local[2].wait()
    local[3].wait()

    hidden = jnp.concatenate([head, tail], axis=0)
    preact = jnp.dot(hidden, weight[...], preferred_element_type=F32)
    sig = jax.nn.sigmoid(preact)
    layer_out[...] = (preact * sig).astype(BF16)
    act = (cot[...].astype(F32) * sig * (1.0 + preact * (1.0 - sig))).astype(BF16)
    hp[z, k, xl] = jnp.dot(weight[...], act.T, preferred_element_type=F32).astype(BF16)

    head_rows, tail_rows = pl.ds(0, B), pl.ds(B, N - B)
    mine = hp.at[z, k, xl]
    mine_head, mine_tail = mine.at[head_rows], mine.at[tail_rows]
    send(mine_tail, mine_tail, "xv", 0, at_x())
    send(mine_head, mine_head, "head", 0, at_z(1))
    send(mine_head, mine_head, "head", 4, at_z(-1))
    send(mine_head, mine_head, "xu", 0, at_x())
    send(mine_tail, mine_tail, "tail", 0, at_z(1))
    send(mine_tail, mine_tail, "tail", 4, at_z(-1))

    def place(d):
        return (z + d + 8) % 8

    def came_from(w, step):
        return place(-1 - step) if w == 0 else place(1 + step)

    def number(d):
        return d if d >= 0 else 8 + d

    def head_step(w, step):
        dist = 4 if step == 3 else (1 + step if w else -1 - step)
        rows = hp.at[came_from(w, step), k, xl, head_rows]
        arrive(rows, "head", w * 4 + step)
        if step < 2 or (step == 2 and w == 0):
            send(rows, rows, "head", w * 4 + step + 1, at_z(1 - 2 * w))
        send(rows, rows, "xu", number(dist), at_x())

    def tail_step(w, step):
        rows = hp.at[came_from(w, step), k, xl, tail_rows]
        arrive(rows, "tail", w * 4 + step)
        if step < 2 or (step == 2 and w == 1):
            send(rows, rows, "tail", w * 4 + step + 1, at_z(1 - 2 * w))

    def part_step(w, step):
        to = at_z(1 - 2 * w)
        block = hp.at[came_from(w, step), k, ox]
        rows = block.at[tail_rows] if step < 3 else block.at[pl.ds(B + w * 64, 64)]
        arrive(rows, "part", w * 4 + step)
        if step < 2:
            send(rows, rows, "part", w * 4 + step + 1, to)
        elif step == 2:
            half = block.at[pl.ds(B + w * 64, 64)]
            send(half, half, "part", w * 4 + 3, to)

    def share(d):
        block = hp.at[place(d), k, ox, head_rows]
        arrive(block, "xu", number(d))
        both = hp.at[place(d), k]
        send(both, both, "pair", number(d), at_core())

    def have(d):
        arrive(hp.at[place(d), ok], "pair", number(d))

    def add_product(where, blocks, n, first=False):
        zt, half, begin = where
        left = jnp.concatenate([hp[zt, u, v] for u, v in blocks], axis=1)
        rows = [
            pair(half + v * 4, begin + u * 32 + 2 * n + q * 16) for u, v in blocks for q in range(2)
        ]
        total = jnp.dot(left, jnp.concatenate(rows, axis=0), preferred_element_type=F32)
        if first:
            acc[n] = total
        else:
            acc[n] += total

    every = [(0, 0), (0, 1), (1, 0), (1, 1)]
    others = [(k, ox), (ok, xl), (ok, ox)]

    def own_block(d):
        where = spot(place(d))

        @pl.loop(0, 8)
        def _(n):
            add_product(where, [(k, xl)], n, d == 0)

    def backward(d, part):
        if part == 0:
            have(d)
        where = spot(place(d))

        @pl.loop(2 * part, 2 * part + 2)
        def _(n):
            add_product(where, others if abs(d) < 2 else every, n)

    def x_tail():
        rows = hp.at[z, k, ox, tail_rows]
        arrive(rows, "xv", 0)
        send(rows, rows, "part", 0, at_z(1))
        send(rows, rows, "part", 4, at_z(-1))

    def gradient_step(step):
        if step == 1:
            w1s[...] = jnp.dot(hidden.T, act, preferred_element_type=F32).reshape(8, 32, N)
            for i in range(1, 8):
                send(w1s.at[row_of(i)], w1r.at[r], "w1", i, at_row(i))
        elif step == 2:
            for i in range(1, 8):
                arrive(w1r.at[row_from(i)], "w1", i)
            w1r[r] = w1s[r]
            s = w1r[0]
            for i in range(1, 8):
                s = s + w1r[i]
            for i in range(8):
                w2s[i] = s[(i // 2) * 8:(i // 2) * 8 + 8, (i % 2) * 128:(i % 2) * 128 + 128]
            for i in range(1, 8):
                send(w2s.at[place(i)], w2r.at[z], "w2", i, at_z(i))
        elif step == 3:
            for i in range(1, 8):
                arrive(w2r.at[place(-i)], "w2", i)
            w2r[z] = w2s[z]
            s = w2r[0]
            for i in range(1, 8):
                s = s + w2r[i]
            w3r[xl * 2 + k] = s
            for i in range(1, 4):
                send(w3r.at[xl * 2 + k], w3r.at[xl * 2 + k], "w3", i, at_mate(i))
        elif step == 4:
            for i in range(1, 4):
                arrive(w3r.at[((xl + i // 2) % 2) * 2 + (k + i % 2) % 2], "w3", i)
            w4r[r] = (w3r[0] + w3r[1]) + (w3r[2] + w3r[3])
            for i in range(1, 8):
                send(w4r.at[r], w4r.at[r], "w4", i, at_row(i))
        else:
            for i in range(1, 8):
                arrive(w4r.at[row_from(i)], "w4", i)
            w5r[z] = w4r[...]
            for i in range(1, 8):
                send(w5r.at[z], w5r.at[z], "w5", i, at_z(i))

    for op in GATHER:
        if op[:2] == "OH":
            head_step(int(op[2]), int(op[3]))
        elif op[:2] == "OT":
            tail_step(int(op[2]), int(op[3]))
        elif op[:2] == "PT":
            part_step(int(op[2]), int(op[3]))
        elif op[:2] == "SH":
            share(int(op[2:]))
        elif op[0] == "B":
            own_block(int(op[1:]))
        elif op[0] == "C":
            d, part = op[1:].split(",")
            backward(int(d), int(part))
        elif op[0] == "W":
            gradient_step(int(op[1]))
        else:
            x_tail()

    have(4)
    farthest = spot(place(4))

    @pl.loop(0, 8)
    def _(j):
        i = (j + 1) % 8
        n = row_of(i)
        add_product(farthest, every, n)

        @pl.when(i != 0)
        def _():
            gs[n] = acc[n].astype(BF16)
            desc(gs.at[n], gr.at[r], "grad", i, at_row(i)).start()

    gradient_step(5)
    s = acc[r]
    for i in range(1, 8):
        arrive(gr.at[row_from(i)], "grad", i)
        s = s + gr[row_from(i)].astype(F32)
    feature_grad[...] = s.T.astype(BF16)
    for i in range(1, 8):
        arrive(w5r.at[place(-i)], "w5", i)
    for i in range(8):
        for j in range(8):
            first = j * 32 + (i // 2) * 8
            weight_grad[first:first + 8, (i % 2) * 128:(i % 2) * 128 + 128] = w5r[i, j] * (65536.0 ** -0.5)
    for d in sent:
        d.wait_send()
    for i in range(1, 8):
        desc(gs.at[row_of(i)], gr.at[r], "grad", i, at_row(i)).wait_send()


def hand_over(a, b, c, a_out, b_out, c_out):
    a_out[...] = a[...]
    b_out[...] = b[...]
    c_out[...] = c[...]


def body(features, edge_tiles, tile_slot, tile_count, weight, cotangent):
    vmem = pl.BlockSpec(memory_space=pltpu.VMEM)

    def buf(*shape, dtype=BF16):
        return pltpu.VMEM(shape, dtype)

    hbm = pl.BlockSpec(memory_space=pl.ANY)
    smem = pl.BlockSpec(memory_space=pltpu.SMEM)
    shapes = (
        jax.ShapeDtypeStruct((N, N), BF16),
        jax.ShapeDtypeStruct((N, N), F32),
        jax.ShapeDtypeStruct((N, N), BF16),
    )
    results = pl.pallas_call(
        kernel,
        out_shape=shapes,
        in_specs=[smem, smem, hbm, hbm, hbm, hbm],
        out_specs=(vmem, vmem, vmem),
        scratch_shapes=[
            buf(193, 128, 128),
            buf(8, N, N),
            buf(8, 2, 2 * N, N, dtype=F32),
            buf(8, 2, N, N),
            buf(8, 2, N, N),
            buf(8, A, N),
            buf(8, A, N, dtype=F32),
            buf(8, A, N),
            buf(7, 2, N - A, N),
            buf(2, 4, 2, N - A, N),
            buf(7, A, N),
            buf(2, 4, A, N),
            buf(N - A, N),
            buf(N - A, N),
            buf(N - A, N, dtype=F32),
            buf(8, 2, 2, N, N),
            buf(8, N, N, dtype=F32),
            buf(8, 32, N, dtype=F32),
            buf(8, 32, N, dtype=F32),
            buf(8, 8, 128, dtype=F32),
            buf(8, 8, 128, dtype=F32),
            buf(4, 8, 128, dtype=F32),
            buf(8, 8, 128, dtype=F32),
            buf(8, 8, 8, 128, dtype=F32),
            buf(8, N, N),
            buf(8, N, N),
            buf(N, N),
            buf(N, N),
            buf(8, 128, dtype=jnp.int32),
            pltpu.SMEM((8, 128), jnp.int32),
            pltpu.SemaphoreType.DMA((TOTAL,)),
            pltpu.SemaphoreType.DMA((TOTAL,)),
            pltpu.SemaphoreType.DMA((5,)),
        ],
        compiler_params=pltpu.CompilerParams(
            collective_id=0, has_side_effects=True, vmem_limit_bytes=56 * 2**20
        ),
    )(tile_slot, tile_count, features, edge_tiles.reshape(192, 128, 128), weight, cotangent)
    return pl.pallas_call(
        hand_over,
        out_shape=shapes,
        in_specs=[vmem] * 3,
        out_specs=(vmem,) * 3,
    )(*results)


def solution(mesh):
    in_specs = (
        P(("col", "row"), None),
        P("row", "col", None, None),
        P("row", "col"),
        P("row", "col"),
        P(),
        P(("row", "col"), None),
    )
    out_specs = (P(("row", "col"), None), P(), P(("col", "row"), None))
    return jax.shard_map(body, mesh=mesh, in_specs=in_specs, out_specs=out_specs, check_vma=False)
```

```python
import functools

import jax
import jax.numpy as jnp
from jax import lax
from jax.experimental import pallas as pl
from jax.experimental.pallas import tpu as pltpu
from jax.sharding import PartitionSpec as P

F32 = jnp.float32
BF16 = jnp.bfloat16
MESH = pl.DeviceIdType.MESH
N = 256
A = 128
B = 128
DIST = (4, 3, -3, 2, -2, 1, -1, 0)
SEMS = dict(
    feat=8, core=8, xrow=8, ringz=16, ringx=8, xfin=1,
    head=8, tail=8, part=8, xv=1, xu=8, pair=8,
    w1=8, w2=8, w3=4, w4=8, w5=8, grad=8,
)
SUMS = (
    "Fa0", "Fb0", "Fa1", "Fb1", "S0", "Z00", "Z01", "Fa2", "S1", "Z11", "Fb2", "Fa3", "S2", "Z20", "Fb3", "X0", "Z10",
    "Z21", "S3", "Fa4", "Fb4", "Z31", "Fa5", "S4", "Z40", "X1", "Fb5", "X2", "S5", "Z30", "Fa6", "Z41", "Fb6", "Z51",
    "Fa7", "S6", "Z60", "X3", "Fb7", "X4", "S7", "Z50", "Z61", "X5", "X6", "P0", "P1", "P2", "P3",
)
GATHER = (
    "B0", "OH00", "OH10", "V", "W1", "OT10", "OT00", "SH0", "B1", "B-1", "C0,0", "C0,1", "OH01", "OH11", "C0,2",
    "C0,3", "PT00", "SH-1", "PT10", "SH1", "OT01", "OT11", "C-1,0", "C-1,1", "W2", "C-1,2", "C-1,3", "OH12", "OH02",
    "C1,0", "C1,1", "PT01", "PT11", "SH-2", "C1,2", "C1,3", "SH2", "OT02", "OT12", "C-2,0", "C-2,1", "OH03", "C-2,2",
    "C-2,3", "C2,0", "PT02", "SH-3", "PT12", "SH3", "C2,1", "C2,2", "OT13", "C2,3", "W3", "C-3,0", "C-3,1", "C-3,2",
    "PT13", "PT03", "SH4", "C-3,3", "W4", "C3,0", "C3,1", "C3,2", "C3,3",
)
OFFSET = {}
TOTAL = 0
for _name, _count in SEMS.items():
    OFFSET[_name] = TOTAL
    TOTAL += _count


def kernel(
    slots, count, feat, tiles_hbm, weight_hbm, cot_hbm,
    layer_out, weight_grad, feature_grad,
    tiles, xpan, pacc, ks, kr, sxs, sx, rx, zs, rz, qs, rq, xfs, xfr, zf,
    hp, acc, w1s, w1r, w2s, w2r, w3r, w4r, w5r, gs, gr, weight, cot, inv_v, inv,
    ssem, rsem, tsem,
):
    r = lax.axis_index("row")
    c = lax.axis_index("col")
    xh, y = r // 4, r % 4
    xl, z, k = c // 16, (c % 16) // 2, c % 2
    ox, ok = 1 - xl, 1 - k

    def row_of(i):
        return ((xh + i // 4) % 2) * 4 + (y + i % 4) % 4

    def row_from(i):
        return ((xh + i // 4) % 2) * 4 + (y + 4 - i % 4) % 4

    def at_row(i):
        return (row_of(i), c)

    def at_z(d):
        return (r, xl * 16 + ((z + d + 8) % 8) * 2 + k)

    def at_x():
        return (r, ox * 16 + z * 2 + k)

    def at_core():
        return (r, xl * 16 + z * 2 + ok)

    def at_mate(i):
        return (r, ((xl + i // 2) % 2) * 16 + z * 2 + (k + i % 2) % 2)

    sent = []

    def desc(src, dst, name, i, to):
        return pltpu.make_async_remote_copy(
            src_ref=src, dst_ref=dst, send_sem=ssem.at[OFFSET[name] + i],
            recv_sem=rsem.at[OFFSET[name] + i], device_id=to, device_id_type=MESH,
        )

    def send(src, dst, name, i, to):
        d = desc(src, dst, name, i, to)
        d.start()
        sent.append(d)

    def arrive(dst, name, i):
        desc(dst, dst, name, i, at_core()).wait_recv()

    barrier = pltpu.get_barrier_semaphore()
    for i in range(1, 8):
        pl.semaphore_signal(barrier, inc=1, device_id=at_row(i), device_id_type=MESH)
        pl.semaphore_signal(barrier, inc=1, device_id=at_z(i), device_id_type=MESH)
    for i in range(1, 4):
        pl.semaphore_signal(barrier, inc=1, device_id=at_mate(i), device_id_type=MESH)
    local = [
        pltpu.make_async_copy(src, dst, tsem.at[i])
        for i, (src, dst) in enumerate((
            (feat, xpan.at[r]), (tiles_hbm, tiles.at[pl.ds(0, 192)]), (weight_hbm, weight), (cot_hbm, cot),
        ))
    ]
    for copy in local:
        copy.start()
    tiles[192] = jnp.zeros((128, 128), BF16)
    cell = lax.broadcasted_iota(jnp.int32, (8, 128), 0) * 128 + lax.broadcasted_iota(jnp.int32, (8, 128), 1)
    live = count[0, 0]

    def find(s, table):
        return jnp.where((cell == slots[0, s]) & (s < live), s, table)

    inv_v[...] = lax.fori_loop(0, 192, find, jnp.full((8, 128), 192, jnp.int32), unroll=8)
    place_table = pltpu.make_async_copy(inv_v, inv, tsem.at[4])
    place_table.start()
    local[0].wait()
    pl.semaphore_wait(barrier, 17)

    for i in (4, 1, 3, 2, 5, 7, 6):
        send(xpan.at[r], xpan.at[r], "feat", i, at_row(i))
    place_table.wait()
    local[1].wait()

    two = jnp.int32(2)

    def spot(zt):
        return zt, lax.div(zt, two), lax.rem(zt, two) * 64

    def pair(n, at):
        return jnp.concatenate([tiles[inv[n, at]], tiles[inv[n, at + 1]]], axis=1)

    def product(where, kt, blocks):
        _, half, begin = where
        begin = begin + kt * 32
        total = None
        for p in blocks:
            at = begin + 2 * p
            rows = [pair(half + (q // 2) * 4, at + (q % 2) * 16) for q in range(4)]
            part = jnp.dot(jnp.concatenate(rows, axis=0), xpan[p], preferred_element_type=F32)
            total = part if total is None else total + part
        return total

    @pl.loop(0, 16)
    def _(j):
        zt, kt = lax.div(j, two), lax.rem(j, two)
        pacc[zt, kt] = product(spot(zt), kt, [r])

    for i in (1, 3, 4):
        arrive(xpan.at[row_from(i)], "feat", i)
    early = [row_from(i) for i in (1, 3, 4)]
    late = [row_from(i) for i in (2, 5, 7, 6)]

    @pl.loop(0, 16)
    def _(j):
        zt, kt = lax.div(j, two), lax.rem(j, two)
        pacc[zt, kt] += product(spot(zt), kt, early)

    for i in (2, 5, 7, 6):
        arrive(xpan.at[row_from(i)], "feat", i)

    def side(q):
        return xl if q else ox

    def forward(g, h):
        zt = (z + DIST[g] + 8) % 8
        kt = k if h else ok
        pacc[zt, kt] += product(spot(zt), kt, late)
        if h == 0:
            for q in range(2):
                ks[g, q] = pacc[zt, kt, pl.ds(q * N, N)].astype(BF16)
            send(ks.at[g], kr.at[g], "core", g, at_core())

    def chip_sum(g, q, first, last):
        zt, x = (z + DIST[g] + 8) % 8, side(q)
        return pacc[zt, k, pl.ds(x * N + first, last - first)] + kr[g, x, first:last].astype(F32)

    def way(d):
        return (0, 4 - d) if d > 0 else (1, 4 + d)

    def chip(g):
        arrive(kr.at[g], "core", g)
        sxs[g] = chip_sum(g, 0, 0, A).astype(BF16)
        send(sxs.at[g], rx.at[g], "xrow", g, at_x())
        sx[g] = chip_sum(g, 1, 0, A)

    def ring_z(g, q):
        s = chip_sum(g, q, A, N)
        w, step = (q, 0) if DIST[g] == 4 else way(DIST[g])
        if step > 1 or (step == 1 and q == w):
            arrive(rz.at[w, step - 1, q], "ringz", (w * 4 + step - 1) * 2 + q)
            s = s + rz[w, step - 1, q].astype(F32)
        zs[g, q] = s.astype(BF16)
        send(zs.at[g, q], rz.at[w, step, q], "ringz", (w * 4 + step) * 2 + q, at_z(1 - 2 * w))

    def ring_x(g):
        d = DIST[g]
        arrive(rx.at[g], "xrow", g)
        s = sx[g] + rx[g].astype(F32)
        if d == 4:
            qs[g] = s.astype(BF16)
            for w in range(2):
                rows = pl.ds(w * (A // 2), A // 2)
                send(qs.at[g, rows], rq.at[w, 0, rows], "ringx", w * 4, at_z(1 - 2 * w))
            return
        w, step = way(d)
        if step == 1:
            rows = pl.ds(w * (A // 2), A // 2)
            arrive(rq.at[w, 0, rows], "ringx", w * 4)
            sx[g] = s
            sx[g, rows] += rq[w, 0, rows].astype(F32)
            s = sx[g]
        else:
            arrive(rq.at[w, step - 1], "ringx", w * 4 + step - 1)
            s = s + rq[w, step - 1].astype(F32)
        qs[g] = s.astype(BF16)
        send(qs.at[g], rq.at[w, step], "ringx", w * 4 + step, at_z(1 - 2 * w))

    def last_z(q):
        for w in range(2):
            arrive(rz.at[w, 3, q], "ringz", (w * 4 + 3) * 2 + q)
        s = chip_sum(7, q, A, N) + rz[0, 3, q].astype(F32) + rz[1, 3, q].astype(F32)
        if q == 0:
            xfs[...] = s.astype(BF16)
            send(xfs, xfr, "xfin", 0, at_x())
        else:
            zf[...] = s

    for op in SUMS:
        if op[:2] == "Fa":
            forward(int(op[2]), 0)
        elif op[:2] == "Fb":
            forward(int(op[2]), 1)
        elif op[0] == "S":
            chip(int(op[1]))
        elif op[0] == "Z":
            ring_z(int(op[1]), int(op[2]))
        elif op[0] == "X":
            ring_x(int(op[1]))
        elif op in ("P0", "P1"):
            last_z(int(op[1]))
    arrive(rx.at[7], "xrow", 7)
    for w in range(2):
        arrive(rq.at[w, 3], "ringx", w * 4 + 3)
    head = (sx[7] + rx[7].astype(F32) + rq[0, 3].astype(F32) + rq[1, 3].astype(F32)).astype(BF16)
    arrive(xfr, "xfin", 0)
    tail = (zf[...] + xfr[...].astype(F32)).astype(BF16)
    local[2].wait()
    local[3].wait()

    hidden = jnp.concatenate([head, tail], axis=0)
    preact = jnp.dot(hidden, weight[...], preferred_element_type=F32)
    sig = jax.nn.sigmoid(preact)
    layer_out[...] = (preact * sig).astype(BF16)
    act = (cot[...].astype(F32) * sig * (1.0 + preact * (1.0 - sig))).astype(BF16)
    hp[z, k, xl] = jnp.dot(weight[...], act.T, preferred_element_type=F32).astype(BF16)

    head_rows, tail_rows = pl.ds(0, B), pl.ds(B, N - B)
    mine = hp.at[z, k, xl]
    mine_head, mine_tail = mine.at[head_rows], mine.at[tail_rows]
    send(mine_tail, mine_tail, "xv", 0, at_x())
    send(mine_head, mine_head, "head", 0, at_z(1))
    send(mine_head, mine_head, "head", 4, at_z(-1))
    send(mine_head, mine_head, "xu", 0, at_x())
    send(mine_tail, mine_tail, "tail", 0, at_z(1))
    send(mine_tail, mine_tail, "tail", 4, at_z(-1))

    def place(d):
        return (z + d + 8) % 8

    def came_from(w, step):
        return place(-1 - step) if w == 0 else place(1 + step)

    def number(d):
        return d if d >= 0 else 8 + d

    def head_step(w, step):
        dist = 4 if step == 3 else (1 + step if w else -1 - step)
        rows = hp.at[came_from(w, step), k, xl, head_rows]
        arrive(rows, "head", w * 4 + step)
        if step < 2 or (step == 2 and w == 0):
            send(rows, rows, "head", w * 4 + step + 1, at_z(1 - 2 * w))
        send(rows, rows, "xu", number(dist), at_x())

    def tail_step(w, step):
        rows = hp.at[came_from(w, step), k, xl, tail_rows]
        arrive(rows, "tail", w * 4 + step)
        if step < 2 or (step == 2 and w == 1):
            send(rows, rows, "tail", w * 4 + step + 1, at_z(1 - 2 * w))

    def part_step(w, step):
        to = at_z(1 - 2 * w)
        block = hp.at[came_from(w, step), k, ox]
        rows = block.at[tail_rows] if step < 3 else block.at[pl.ds(B + w * 64, 64)]
        arrive(rows, "part", w * 4 + step)
        if step < 2:
            send(rows, rows, "part", w * 4 + step + 1, to)
        elif step == 2:
            half = block.at[pl.ds(B + w * 64, 64)]
            send(half, half, "part", w * 4 + 3, to)

    def share(d):
        block = hp.at[place(d), k, ox, head_rows]
        arrive(block, "xu", number(d))
        both = hp.at[place(d), k]
        send(both, both, "pair", number(d), at_core())

    def have(d):
        arrive(hp.at[place(d), ok], "pair", number(d))

    def add_products(where, blocks, places, first=False):
        zt, half, begin = where
        left = jnp.concatenate([hp[zt, u, v] for u, v in blocks], axis=1)
        totals = []
        for n in places:
            rows = [
                pair(half + v * 4, begin + u * 32 + 2 * n + q * 16) for u, v in blocks for q in range(2)
            ]
            totals.append(jnp.dot(left, jnp.concatenate(rows, axis=0), preferred_element_type=F32))
        for n, total in zip(places, totals):
            if first:
                acc[n] = total
            else:
                acc[n] += total

    every = [(0, 0), (0, 1), (1, 0), (1, 1)]
    others = [(k, ox), (ok, xl), (ok, ox)]

    def own_block(d):
        where = spot(place(d))

        for n in (0, 4):
            add_products(where, [(k, xl)], [n, n + 1, n + 2, n + 3], d == 0)

    def backward(d, part):
        if part == 0:
            have(d)
        where = spot(place(d))
        add_products(where, others if abs(d) < 2 else every, [2 * part, 2 * part + 1])

    def x_tail():
        rows = hp.at[z, k, ox, tail_rows]
        arrive(rows, "xv", 0)
        send(rows, rows, "part", 0, at_z(1))
        send(rows, rows, "part", 4, at_z(-1))

    def gradient_step(step):
        if step == 1:
            w1s[...] = jnp.dot(hidden.T, act, preferred_element_type=F32).reshape(8, 32, N)
            for i in range(1, 8):
                send(w1s.at[row_of(i)], w1r.at[r], "w1", i, at_row(i))
        elif step == 2:
            for i in range(1, 8):
                arrive(w1r.at[row_from(i)], "w1", i)
            w1r[r] = w1s[r]
            s = w1r[0]
            for i in range(1, 8):
                s = s + w1r[i]
            for i in range(8):
                w2s[i] = s[(i // 2) * 8:(i // 2) * 8 + 8, (i % 2) * 128:(i % 2) * 128 + 128]
            for i in range(1, 8):
                send(w2s.at[place(i)], w2r.at[z], "w2", i, at_z(i))
        elif step == 3:
            for i in range(1, 8):
                arrive(w2r.at[place(-i)], "w2", i)
            w2r[z] = w2s[z]
            s = w2r[0]
            for i in range(1, 8):
                s = s + w2r[i]
            w3r[xl * 2 + k] = s
            for i in range(1, 4):
                send(w3r.at[xl * 2 + k], w3r.at[xl * 2 + k], "w3", i, at_mate(i))
        elif step == 4:
            for i in range(1, 4):
                arrive(w3r.at[((xl + i // 2) % 2) * 2 + (k + i % 2) % 2], "w3", i)
            w4r[r] = (w3r[0] + w3r[1]) + (w3r[2] + w3r[3])
            for i in range(1, 8):
                send(w4r.at[r], w4r.at[r], "w4", i, at_row(i))
        else:
            for i in range(1, 8):
                arrive(w4r.at[row_from(i)], "w4", i)
            w5r[z] = w4r[...]
            for i in range(1, 8):
                send(w5r.at[z], w5r.at[z], "w5", i, at_z(i))

    for op in GATHER:
        if op[:2] == "OH":
            head_step(int(op[2]), int(op[3]))
        elif op[:2] == "OT":
            tail_step(int(op[2]), int(op[3]))
        elif op[:2] == "PT":
            part_step(int(op[2]), int(op[3]))
        elif op[:2] == "SH":
            share(int(op[2:]))
        elif op[0] == "B":
            own_block(int(op[1:]))
        elif op[0] == "C":
            d, part = op[1:].split(",")
            backward(int(d), int(part))
        elif op[0] == "W":
            gradient_step(int(op[1]))
        else:
            x_tail()

    have(4)
    farthest = spot(place(4))

    for group in ((6, 5), (7, 2), (4, 1), (3, 0)):
        add_products(farthest, every, [row_of(i) for i in group])
        for i in group:
            if i:
                gs[row_of(i)] = acc[row_of(i)].astype(BF16)
                send(gs.at[row_of(i)], gr.at[r], "grad", i, at_row(i))

    gradient_step(5)
    s = acc[r]
    for i in range(1, 8):
        arrive(gr.at[row_from(i)], "grad", i)
        s = s + gr[row_from(i)].astype(F32)
    feature_grad[...] = s.T.astype(BF16)
    for i in range(1, 8):
        arrive(w5r.at[place(-i)], "w5", i)
    for i in range(8):
        for j in range(8):
            first = j * 32 + (i // 2) * 8
            weight_grad[first:first + 8, (i % 2) * 128:(i % 2) * 128 + 128] = w5r[i, j] * (65536.0 ** -0.5)
    for d in sent:
        d.wait_send()


def hand_over(a, b, c, a_out, b_out, c_out):
    a_out[...] = a[...]
    b_out[...] = b[...]
    c_out[...] = c[...]


def body(features, edge_tiles, tile_slot, tile_count, weight, cotangent):
    vmem = pl.BlockSpec(memory_space=pltpu.VMEM)

    def buf(*shape, dtype=BF16):
        return pltpu.VMEM(shape, dtype)

    hbm = pl.BlockSpec(memory_space=pl.ANY)
    smem = pl.BlockSpec(memory_space=pltpu.SMEM)
    shapes = (
        jax.ShapeDtypeStruct((N, N), BF16),
        jax.ShapeDtypeStruct((N, N), F32),
        jax.ShapeDtypeStruct((N, N), BF16),
    )
    results = pl.pallas_call(
        kernel,
        out_shape=shapes,
        in_specs=[smem, smem, hbm, hbm, hbm, hbm],
        out_specs=(vmem, vmem, vmem),
        scratch_shapes=[
            buf(193, 128, 128),
            buf(8, N, N),
            buf(8, 2, 2 * N, N, dtype=F32),
            buf(8, 2, N, N),
            buf(8, 2, N, N),
            buf(8, A, N),
            buf(8, A, N, dtype=F32),
            buf(8, A, N),
            buf(7, 2, N - A, N),
            buf(2, 4, 2, N - A, N),
            buf(7, A, N),
            buf(2, 4, A, N),
            buf(N - A, N),
            buf(N - A, N),
            buf(N - A, N, dtype=F32),
            buf(8, 2, 2, N, N),
            buf(8, N, N, dtype=F32),
            buf(8, 32, N, dtype=F32),
            buf(8, 32, N, dtype=F32),
            buf(8, 8, 128, dtype=F32),
            buf(8, 8, 128, dtype=F32),
            buf(4, 8, 128, dtype=F32),
            buf(8, 8, 128, dtype=F32),
            buf(8, 8, 8, 128, dtype=F32),
            buf(8, N, N),
            buf(8, N, N),
            buf(N, N),
            buf(N, N),
            buf(8, 128, dtype=jnp.int32),
            pltpu.SMEM((8, 128), jnp.int32),
            pltpu.SemaphoreType.DMA((TOTAL,)),
            pltpu.SemaphoreType.DMA((TOTAL,)),
            pltpu.SemaphoreType.DMA((5,)),
        ],
        compiler_params=pltpu.CompilerParams(
            collective_id=0, has_side_effects=True, vmem_limit_bytes=56 * 2**20
        ),
    )(tile_slot, tile_count, features, edge_tiles.reshape(192, 128, 128), weight, cotangent)
    return pl.pallas_call(
        hand_over,
        out_shape=shapes,
        in_specs=[vmem] * 3,
        out_specs=(vmem,) * 3,
    )(*results)


def solution(mesh):
    in_specs = (
        P(("col", "row"), None),
        P("row", "col", None, None),
        P("row", "col"),
        P("row", "col"),
        P(),
        P(("row", "col"), None),
    )
    out_specs = (P(("row", "col"), None), P(), P(("col", "row"), None))
    return jax.shard_map(body, mesh=mesh, in_specs=in_specs, out_specs=out_specs, check_vma=False)
```

```python
import functools

import jax
import jax.numpy as jnp
from jax import lax
from jax.experimental import pallas as pl
from jax.experimental.pallas import tpu as pltpu
from jax.sharding import PartitionSpec as P

F32 = jnp.float32
BF16 = jnp.bfloat16
MESH = pl.DeviceIdType.MESH
N = 256
A = 128
B = 128
DIST = (4, 3, -3, 2, -2, 1, -1, 0)
SEMS = dict(
    feat=12, core=8, xrow=8, ringz=16, ringx=8, xfin=1,
    head=8, tail=8, part=8, xv=1, xu=8, pair=8,
    w1=8, w2=8, w3=4, w4=8, w5=8, grad=8,
)
SUMS = (
    "Fa0", "Fb0", "Fa1", "Fb1", "S0", "Z00", "Z01", "Fa2", "S1", "Z11", "Fb2", "Fa3", "S2", "Z20", "Fb3", "X0", "Z10",
    "Z21", "S3", "Fa4", "Fb4", "Z31", "Fa5", "S4", "Z40", "X1", "Fb5", "X2", "S5", "Z30", "Fa6", "Z41", "Fb6", "Z51",
    "Fa7", "S6", "Z60", "X3", "Fb7", "X4", "S7", "Z50", "Z61", "X5", "X6", "P0", "P1", "P2", "P3",
)
GATHER = (
    "B0", "OH00", "OH10", "V", "W1", "OT10", "OT00", "SH0", "B1", "B-1", "C0,0", "C0,1", "OH01", "OH11", "C0,2",
    "C0,3", "PT00", "SH-1", "PT10", "SH1", "OT01", "OT11", "C-1,0", "C-1,1", "W2", "C-1,2", "C-1,3", "OH12", "OH02",
    "C1,0", "C1,1", "PT01", "PT11", "SH-2", "C1,2", "C1,3", "SH2", "OT02", "OT12", "C-2,0", "C-2,1", "OH03", "C-2,2",
    "C-2,3", "C2,0", "PT02", "SH-3", "PT12", "SH3", "C2,1", "C2,2", "OT13", "C2,3", "W3", "C-3,0", "C-3,1", "C-3,2",
    "PT13", "PT03", "SH4", "C-3,3", "W4", "C3,0", "C3,1", "C3,2", "C3,3",
)
OFFSET = {}
TOTAL = 0
for _name, _count in SEMS.items():
    OFFSET[_name] = TOTAL
    TOTAL += _count


def kernel(
    slots, count, feat, tiles_hbm, weight_hbm, cot_hbm,
    layer_out, weight_grad, feature_grad,
    tiles, xpan, pacc, ks, kr, sxs, sx, rx, zs, rz, qs, rq, xfs, xfr, zf,
    hp, acc, w1s, w1r, w2s, w2r, w3r, w4r, w5r, gs, gr, weight, cot, inv_v, inv,
    ssem, rsem, tsem,
):
    r = lax.axis_index("row")
    c = lax.axis_index("col")
    xh, y = r // 4, r % 4
    xl, z, k = c // 16, (c % 16) // 2, c % 2
    ox, ok = 1 - xl, 1 - k

    def row_of(i):
        return ((xh + i // 4) % 2) * 4 + (y + i % 4) % 4

    def row_from(i):
        return ((xh + i // 4) % 2) * 4 + (y + 4 - i % 4) % 4

    def at_row(i):
        return (row_of(i), c)

    def at_z(d):
        return (r, xl * 16 + ((z + d + 8) % 8) * 2 + k)

    def at_x():
        return (r, ox * 16 + z * 2 + k)

    def at_core():
        return (r, xl * 16 + z * 2 + ok)

    def at_mate(i):
        return (r, ((xl + i // 2) % 2) * 16 + z * 2 + (k + i % 2) % 2)

    sent = []

    def desc(src, dst, name, i, to):
        return pltpu.make_async_remote_copy(
            src_ref=src, dst_ref=dst, send_sem=ssem.at[OFFSET[name] + i],
            recv_sem=rsem.at[OFFSET[name] + i], device_id=to, device_id_type=MESH,
        )

    def send(src, dst, name, i, to):
        d = desc(src, dst, name, i, to)
        d.start()
        sent.append(d)

    def arrive(dst, name, i):
        desc(dst, dst, name, i, at_core()).wait_recv()

    barrier = pltpu.get_barrier_semaphore()
    for i in range(1, 8):
        pl.semaphore_signal(barrier, inc=1, device_id=at_row(i), device_id_type=MESH)
        pl.semaphore_signal(barrier, inc=1, device_id=at_z(i), device_id_type=MESH)
    for i in range(1, 4):
        pl.semaphore_signal(barrier, inc=1, device_id=at_mate(i), device_id_type=MESH)
    local = [
        pltpu.make_async_copy(src, dst, tsem.at[i])
        for i, (src, dst) in enumerate((
            (feat, xpan.at[r]), (tiles_hbm, tiles.at[pl.ds(0, 192)]), (weight_hbm, weight), (cot_hbm, cot),
        ))
    ]
    for copy in local:
        copy.start()
    tiles[192] = jnp.zeros((128, 128), BF16)
    cell = lax.broadcasted_iota(jnp.int32, (8, 128), 0) * 128 + lax.broadcasted_iota(jnp.int32, (8, 128), 1)
    live = count[0, 0]

    def find(s, table):
        return jnp.where((cell == slots[0, s]) & (s < live), s, table)

    inv_v[...] = lax.fori_loop(0, 192, find, jnp.full((8, 128), 192, jnp.int32), unroll=8)
    place_table = pltpu.make_async_copy(inv_v, inv, tsem.at[4])
    place_table.start()
    local[0].wait()
    pl.semaphore_wait(barrier, 17)

    def feature(i, lower=None):
        block = xpan.at[row_from(i)]
        return block if lower is None else block.at[pl.ds(128 * lower, 128)]

    def pass_on(i, lower, name, to):
        send(feature(i, lower), feature(i, lower), "feat", name, at_row(to))

    pass_on(0, 1, 0, 4)
    for i in (1, 3, 2):
        pass_on(0, None, i, i)
    pass_on(0, 0, 4, 4)
    place_table.wait()
    local[1].wait()

    two = jnp.int32(2)

    def spot(zt):
        return zt, lax.div(zt, two), lax.rem(zt, two) * 64

    def pair(n, at):
        return jnp.concatenate([tiles[inv[n, at]], tiles[inv[n, at + 1]]], axis=1)

    def product(where, kt, blocks):
        _, half, begin = where
        begin = begin + kt * 32
        total = None
        for p in blocks:
            at = begin + 2 * p
            rows = [pair(half + (q // 2) * 4, at + (q % 2) * 16) for q in range(4)]
            part = jnp.dot(jnp.concatenate(rows, axis=0), xpan[p], preferred_element_type=F32)
            total = part if total is None else total + part
        return total

    @pl.loop(0, 16)
    def _(j):
        zt, kt = lax.div(j, two), lax.rem(j, two)
        pacc[zt, kt] = product(spot(zt), kt, [r])

    arrive(feature(4, 1), "feat", 0)
    for i in (1, 3, 2):
        pass_on(4, 1, 4 + i, i)
    for i in (1, 3):
        arrive(feature(i), "feat", i)
        pass_on(i, 0, 8 + i, 4)
    late = [row_from(i) for i in (4, 5, 7, 6)]

    def add_early(first, last, places):
        @pl.loop(first, last)
        def _(j):
            zt, kt = lax.div(j, two), lax.rem(j, two)
            pacc[zt, kt] += product(spot(zt), kt, [row_from(i) for i in places])

    add_early(0, 8, (1, 3))
    arrive(feature(2), "feat", 2)
    pass_on(2, 0, 10, 4)
    add_early(8, 16, (1, 3))
    add_early(0, 16, (2,))
    arrive(feature(4, 0), "feat", 4)
    for i in (1, 3, 2):
        arrive(feature(4 + i, 1), "feat", 4 + i)
        arrive(feature(4 + i, 0), "feat", 8 + i)

    def side(q):
        return xl if q else ox

    def forward(g, h):
        zt = (z + DIST[g] + 8) % 8
        kt = k if h else ok
        pacc[zt, kt] += product(spot(zt), kt, late)
        if h == 0:
            for q in range(2):
                ks[g, q] = pacc[zt, kt, pl.ds(q * N, N)].astype(BF16)
            send(ks.at[g], kr.at[g], "core", g, at_core())

    def chip_sum(g, q, first, last):
        zt, x = (z + DIST[g] + 8) % 8, side(q)
        return pacc[zt, k, pl.ds(x * N + first, last - first)] + kr[g, x, first:last].astype(F32)

    def way(d):
        return (0, 4 - d) if d > 0 else (1, 4 + d)

    def chip(g):
        arrive(kr.at[g], "core", g)
        sxs[g] = chip_sum(g, 0, 0, A).astype(BF16)
        send(sxs.at[g], rx.at[g], "xrow", g, at_x())
        sx[g] = chip_sum(g, 1, 0, A)

    def ring_z(g, q):
        s = chip_sum(g, q, A, N)
        w, step = (q, 0) if DIST[g] == 4 else way(DIST[g])
        if step > 1 or (step == 1 and q == w):
            arrive(rz.at[w, step - 1, q], "ringz", (w * 4 + step - 1) * 2 + q)
            s = s + rz[w, step - 1, q].astype(F32)
        zs[g, q] = s.astype(BF16)
        send(zs.at[g, q], rz.at[w, step, q], "ringz", (w * 4 + step) * 2 + q, at_z(1 - 2 * w))

    def ring_x(g):
        d = DIST[g]
        arrive(rx.at[g], "xrow", g)
        s = sx[g] + rx[g].astype(F32)
        if d == 4:
            qs[g] = s.astype(BF16)
            for w in range(2):
                rows = pl.ds(w * (A // 2), A // 2)
                send(qs.at[g, rows], rq.at[w, 0, rows], "ringx", w * 4, at_z(1 - 2 * w))
            return
        w, step = way(d)
        if step == 1:
            rows = pl.ds(w * (A // 2), A // 2)
            arrive(rq.at[w, 0, rows], "ringx", w * 4)
            sx[g] = s
            sx[g, rows] += rq[w, 0, rows].astype(F32)
            s = sx[g]
        else:
            arrive(rq.at[w, step - 1], "ringx", w * 4 + step - 1)
            s = s + rq[w, step - 1].astype(F32)
        qs[g] = s.astype(BF16)
        send(qs.at[g], rq.at[w, step], "ringx", w * 4 + step, at_z(1 - 2 * w))

    def last_z(q):
        for w in range(2):
            arrive(rz.at[w, 3, q], "ringz", (w * 4 + 3) * 2 + q)
        s = chip_sum(7, q, A, N) + rz[0, 3, q].astype(F32) + rz[1, 3, q].astype(F32)
        if q == 0:
            xfs[...] = s.astype(BF16)
            send(xfs, xfr, "xfin", 0, at_x())
        else:
            zf[...] = s

    for op in SUMS:
        if op[:2] == "Fa":
            forward(int(op[2]), 0)
        elif op[:2] == "Fb":
            forward(int(op[2]), 1)
        elif op[0] == "S":
            chip(int(op[1]))
        elif op[0] == "Z":
            ring_z(int(op[1]), int(op[2]))
        elif op[0] == "X":
            ring_x(int(op[1]))
        elif op in ("P0", "P1"):
            last_z(int(op[1]))
    arrive(rx.at[7], "xrow", 7)
    for w in range(2):
        arrive(rq.at[w, 3], "ringx", w * 4 + 3)
    head = (sx[7] + rx[7].astype(F32) + rq[0, 3].astype(F32) + rq[1, 3].astype(F32)).astype(BF16)
    arrive(xfr, "xfin", 0)
    tail = (zf[...] + xfr[...].astype(F32)).astype(BF16)
    local[2].wait()
    local[3].wait()

    hidden = jnp.concatenate([head, tail], axis=0)
    preact = jnp.dot(hidden, weight[...], preferred_element_type=F32)
    sig = jax.nn.sigmoid(preact)
    layer_out[...] = (preact * sig).astype(BF16)
    act = (cot[...].astype(F32) * sig * (1.0 + preact * (1.0 - sig))).astype(BF16)
    hp[z, k, xl] = jnp.dot(weight[...], act.T, preferred_element_type=F32).astype(BF16)

    head_rows, tail_rows = pl.ds(0, B), pl.ds(B, N - B)
    mine = hp.at[z, k, xl]
    mine_head, mine_tail = mine.at[head_rows], mine.at[tail_rows]
    send(mine_tail, mine_tail, "xv", 0, at_x())
    send(mine_head, mine_head, "head", 0, at_z(1))
    send(mine_head, mine_head, "head", 4, at_z(-1))
    send(mine_head, mine_head, "xu", 0, at_x())
    send(mine_tail, mine_tail, "tail", 0, at_z(1))
    send(mine_tail, mine_tail, "tail", 4, at_z(-1))

    def place(d):
        return (z + d + 8) % 8

    def came_from(w, step):
        return place(-1 - step) if w == 0 else place(1 + step)

    def number(d):
        return d if d >= 0 else 8 + d

    def head_step(w, step):
        dist = 4 if step == 3 else (1 + step if w else -1 - step)
        rows = hp.at[came_from(w, step), k, xl, head_rows]
        arrive(rows, "head", w * 4 + step)
        if step < 2 or (step == 2 and w == 0):
            send(rows, rows, "head", w * 4 + step + 1, at_z(1 - 2 * w))
        send(rows, rows, "xu", number(dist), at_x())

    def tail_step(w, step):
        rows = hp.at[came_from(w, step), k, xl, tail_rows]
        arrive(rows, "tail", w * 4 + step)
        if step < 2 or (step == 2 and w == 1):
            send(rows, rows, "tail", w * 4 + step + 1, at_z(1 - 2 * w))

    def part_step(w, step):
        to = at_z(1 - 2 * w)
        block = hp.at[came_from(w, step), k, ox]
        rows = block.at[tail_rows] if step < 3 else block.at[pl.ds(B + w * 64, 64)]
        arrive(rows, "part", w * 4 + step)
        if step < 2:
            send(rows, rows, "part", w * 4 + step + 1, to)
        elif step == 2:
            half = block.at[pl.ds(B + w * 64, 64)]
            send(half, half, "part", w * 4 + 3, to)

    def share(d):
        block = hp.at[place(d), k, ox, head_rows]
        arrive(block, "xu", number(d))
        both = hp.at[place(d), k]
        send(both, both, "pair", number(d), at_core())

    def have(d):
        arrive(hp.at[place(d), ok], "pair", number(d))

    def add_products(where, blocks, places, first=False):
        zt, half, begin = where
        left = jnp.concatenate([hp[zt, u, v] for u, v in blocks], axis=1)
        totals = []
        for n in places:
            rows = [
                pair(half + v * 4, begin + u * 32 + 2 * n + q * 16) for u, v in blocks for q in range(2)
            ]
            totals.append(jnp.dot(left, jnp.concatenate(rows, axis=0), preferred_element_type=F32))
        for n, total in zip(places, totals):
            if first:
                acc[n] = total
            else:
                acc[n] += total

    every = [(0, 0), (0, 1), (1, 0), (1, 1)]
    others = [(k, ox), (ok, xl), (ok, ox)]

    def own_block(d):
        where = spot(place(d))

        for n in (0, 4):
            add_products(where, [(k, xl)], [n, n + 1, n + 2, n + 3], d == 0)

    def backward(d, part):
        if part == 0:
            have(d)
        where = spot(place(d))
        add_products(where, others if abs(d) < 2 else every, [2 * part, 2 * part + 1])

    def x_tail():
        rows = hp.at[z, k, ox, tail_rows]
        arrive(rows, "xv", 0)
        send(rows, rows, "part", 0, at_z(1))
        send(rows, rows, "part", 4, at_z(-1))

    def gradient_step(step):
        if step == 1:
            w1s[...] = jnp.dot(hidden.T, act, preferred_element_type=F32).reshape(8, 32, N)
            for i in range(1, 8):
                send(w1s.at[row_of(i)], w1r.at[r], "w1", i, at_row(i))
        elif step == 2:
            for i in range(1, 8):
                arrive(w1r.at[row_from(i)], "w1", i)
            w1r[r] = w1s[r]
            s = w1r[0]
            for i in range(1, 8):
                s = s + w1r[i]
            for i in range(8):
                w2s[i] = s[(i // 2) * 8:(i // 2) * 8 + 8, (i % 2) * 128:(i % 2) * 128 + 128]
            for i in range(1, 8):
                send(w2s.at[place(i)], w2r.at[z], "w2", i, at_z(i))
        elif step == 3:
            for i in range(1, 8):
                arrive(w2r.at[place(-i)], "w2", i)
            w2r[z] = w2s[z]
            s = w2r[0]
            for i in range(1, 8):
                s = s + w2r[i]
            w3r[xl * 2 + k] = s
            for i in range(1, 4):
                send(w3r.at[xl * 2 + k], w3r.at[xl * 2 + k], "w3", i, at_mate(i))
        elif step == 4:
            for i in range(1, 4):
                arrive(w3r.at[((xl + i // 2) % 2) * 2 + (k + i % 2) % 2], "w3", i)
            w4r[r] = (w3r[0] + w3r[1]) + (w3r[2] + w3r[3])
            for i in range(1, 8):
                send(w4r.at[r], w4r.at[r], "w4", i, at_row(i))
        else:
            for i in range(1, 8):
                arrive(w4r.at[row_from(i)], "w4", i)
            w5r[z] = w4r[...]
            for i in range(1, 8):
                send(w5r.at[z], w5r.at[z], "w5", i, at_z(i))

    for op in GATHER:
        if op[:2] == "OH":
            head_step(int(op[2]), int(op[3]))
        elif op[:2] == "OT":
            tail_step(int(op[2]), int(op[3]))
        elif op[:2] == "PT":
            part_step(int(op[2]), int(op[3]))
        elif op[:2] == "SH":
            share(int(op[2:]))
        elif op[0] == "B":
            own_block(int(op[1:]))
        elif op[0] == "C":
            d, part = op[1:].split(",")
            backward(int(d), int(part))
        elif op[0] == "W":
            gradient_step(int(op[1]))
        else:
            x_tail()

    have(4)
    farthest = spot(place(4))

    for group in ((6, 5), (7, 2), (4, 1), (3, 0)):
        add_products(farthest, every, [row_of(i) for i in group])
        for i in group:
            if i:
                gs[row_of(i)] = acc[row_of(i)].astype(BF16)
                send(gs.at[row_of(i)], gr.at[r], "grad", i, at_row(i))

    gradient_step(5)
    s = acc[r]
    for i in (6, 5, 7, 2, 4, 1, 3):
        arrive(gr.at[row_from(i)], "grad", i)
        s = s + gr[row_from(i)].astype(F32)
    feature_grad[...] = s.astype(BF16).T
    for i in range(1, 8):
        arrive(w5r.at[place(-i)], "w5", i)
    for i in range(8):
        for j in range(8):
            first = j * 32 + (i // 2) * 8
            weight_grad[first:first + 8, (i % 2) * 128:(i % 2) * 128 + 128] = w5r[i, j] * (65536.0 ** -0.5)
    for d in sent:
        d.wait_send()


def hand_over(a, b, c, a_out, b_out, c_out):
    a_out[...] = a[...]
    b_out[...] = b[...]
    c_out[...] = c[...]


def body(features, edge_tiles, tile_slot, tile_count, weight, cotangent):
    vmem = pl.BlockSpec(memory_space=pltpu.VMEM)

    def buf(*shape, dtype=BF16):
        return pltpu.VMEM(shape, dtype)

    hbm = pl.BlockSpec(memory_space=pl.ANY)
    smem = pl.BlockSpec(memory_space=pltpu.SMEM)
    shapes = (
        jax.ShapeDtypeStruct((N, N), BF16),
        jax.ShapeDtypeStruct((N, N), F32),
        jax.ShapeDtypeStruct((N, N), BF16),
    )
    results = pl.pallas_call(
        kernel,
        out_shape=shapes,
        in_specs=[smem, smem, hbm, hbm, hbm, hbm],
        out_specs=(vmem, vmem, vmem),
        scratch_shapes=[
            buf(193, 128, 128),
            buf(8, N, N),
            buf(8, 2, 2 * N, N, dtype=F32),
            buf(8, 2, N, N),
            buf(8, 2, N, N),
            buf(8, A, N),
            buf(8, A, N, dtype=F32),
            buf(8, A, N),
            buf(7, 2, N - A, N),
            buf(2, 4, 2, N - A, N),
            buf(7, A, N),
            buf(2, 4, A, N),
            buf(N - A, N),
            buf(N - A, N),
            buf(N - A, N, dtype=F32),
            buf(8, 2, 2, N, N),
            buf(8, N, N, dtype=F32),
            buf(8, 32, N, dtype=F32),
            buf(8, 32, N, dtype=F32),
            buf(8, 8, 128, dtype=F32),
            buf(8, 8, 128, dtype=F32),
            buf(4, 8, 128, dtype=F32),
            buf(8, 8, 128, dtype=F32),
            buf(8, 8, 8, 128, dtype=F32),
            buf(8, N, N),
            buf(8, N, N),
            buf(N, N),
            buf(N, N),
            buf(8, 128, dtype=jnp.int32),
            pltpu.SMEM((8, 128), jnp.int32),
            pltpu.SemaphoreType.DMA((TOTAL,)),
            pltpu.SemaphoreType.DMA((TOTAL,)),
            pltpu.SemaphoreType.DMA((5,)),
        ],
        compiler_params=pltpu.CompilerParams(
            collective_id=0, has_side_effects=True, vmem_limit_bytes=56 * 2**20
        ),
    )(tile_slot, tile_count, features, edge_tiles.reshape(192, 128, 128), weight, cotangent)
    return pl.pallas_call(
        hand_over,
        out_shape=shapes,
        in_specs=[vmem] * 3,
        out_specs=(vmem,) * 3,
    )(*results)


def solution(mesh):
    in_specs = (
        P(("col", "row"), None),
        P("row", "col", None, None),
        P("row", "col"),
        P("row", "col"),
        P(),
        P(("row", "col"), None),
    )
    out_specs = (P(("row", "col"), None), P(), P(("col", "row"), None))
    return jax.shard_map(body, mesh=mesh, in_specs=in_specs, out_specs=out_specs, check_vma=False)
```

```python
import functools

import jax
import jax.numpy as jnp
from jax import lax
from jax.experimental import pallas as pl
from jax.experimental.pallas import tpu as pltpu
from jax.sharding import PartitionSpec as P

F32 = jnp.float32
BF16 = jnp.bfloat16
MESH = pl.DeviceIdType.MESH
N = 256
A = 128
B = 128
DIST = (4, 3, -3, 2, -2, 1, -1, 0)
SEMS = dict(
    feat=12, core=8, xrow=8, ringz=16, ringx=8, xfin=1,
    head=8, tail=8, part=8, xv=1, xu=8, pair=8,
    w1=8, w2=8, w3=4, w4=8, w5=8, grad=8,
)
SUMS = (
    "Fa0", "Fb0", "Fa1", "Fb1", "S0", "Z00", "Z01", "Fa2", "S1", "Z11", "Fb2", "Fa3", "S2", "Z20", "Fb3", "X0", "Z10",
    "Z21", "S3", "Fa4", "Fb4", "Z31", "Fa5", "S4", "Z40", "X1", "Fb5", "X2", "S5", "Z30", "Fa6", "Z41", "Fb6", "Z51",
    "Fa7", "S6", "Z60", "X3", "Fb7", "X4", "S7", "Z50", "Z61", "X5", "X6", "P0", "P1", "P2", "P3",
)
GATHER = (
    "B0", "OH00", "OH10", "V", "W1", "OT10", "OT00", "SH0", "B1", "B-1", "C0,0", "C0,1", "OH01", "OH11", "C0,2",
    "C0,3", "PT00", "SH-1", "PT10", "SH1", "OT01", "OT11", "C-1,0", "C-1,1", "W2", "C-1,2", "C-1,3", "OH12", "OH02",
    "C1,0", "C1,1", "PT01", "PT11", "SH-2", "C1,2", "C1,3", "SH2", "OT02", "OT12", "C-2,0", "C-2,1", "OH03", "C-2,2",
    "C-2,3", "C2,0", "PT02", "SH-3", "PT12", "SH3", "C2,1", "C2,2", "OT13", "C2,3", "W3", "C-3,0", "C-3,1", "C-3,2",
    "PT13", "PT03", "SH4", "C-3,3", "W4",
)
OFFSET = {}
TOTAL = 0
for _name, _count in SEMS.items():
    OFFSET[_name] = TOTAL
    TOTAL += _count


def kernel(
    slots, count, feat, tiles_hbm, weight_hbm, cot_hbm,
    layer_out, weight_grad, feature_grad,
    tiles, xpan, pacc, ks, kr, sxs, sx, rx, zs, rz, qs, rq, xfs, xfr, zf,
    hp, acc, w1s, w1r, w2s, w2r, w3r, w4r, w5r, gs, gr, weight, cot, inv_v, inv,
    ssem, rsem, tsem,
):
    r = lax.axis_index("row")
    c = lax.axis_index("col")
    xh, y = r // 4, r % 4
    xl, z, k = c // 16, (c % 16) // 2, c % 2
    ox, ok = 1 - xl, 1 - k

    def row_of(i):
        return ((xh + i // 4) % 2) * 4 + (y + i % 4) % 4

    def row_from(i):
        return ((xh + i // 4) % 2) * 4 + (y + 4 - i % 4) % 4

    def at_row(i):
        return (row_of(i), c)

    def at_z(d):
        return (r, xl * 16 + ((z + d + 8) % 8) * 2 + k)

    def at_x():
        return (r, ox * 16 + z * 2 + k)

    def at_core():
        return (r, xl * 16 + z * 2 + ok)

    def at_mate(i):
        return (r, ((xl + i // 2) % 2) * 16 + z * 2 + (k + i % 2) % 2)

    sent = []

    def desc(src, dst, name, i, to):
        return pltpu.make_async_remote_copy(
            src_ref=src, dst_ref=dst, send_sem=ssem.at[OFFSET[name] + i],
            recv_sem=rsem.at[OFFSET[name] + i], device_id=to, device_id_type=MESH,
        )

    def send(src, dst, name, i, to):
        d = desc(src, dst, name, i, to)
        d.start()
        sent.append(d)

    def arrive(dst, name, i):
        desc(dst, dst, name, i, at_core()).wait_recv()

    barrier = pltpu.get_barrier_semaphore()
    for i in range(1, 8):
        pl.semaphore_signal(barrier, inc=1, device_id=at_row(i), device_id_type=MESH)
        pl.semaphore_signal(barrier, inc=1, device_id=at_z(i), device_id_type=MESH)
    for i in range(1, 4):
        pl.semaphore_signal(barrier, inc=1, device_id=at_mate(i), device_id_type=MESH)
    local = [
        pltpu.make_async_copy(src, dst, tsem.at[i])
        for i, (src, dst) in enumerate((
            (feat, xpan.at[r]), (tiles_hbm, tiles.at[pl.ds(0, 192)]), (weight_hbm, weight), (cot_hbm, cot),
        ))
    ]
    for copy in local:
        copy.start()
    tiles[192] = jnp.zeros((128, 128), BF16)
    cell = lax.broadcasted_iota(jnp.int32, (8, 128), 0) * 128 + lax.broadcasted_iota(jnp.int32, (8, 128), 1)
    live = count[0, 0]

    def find(s, table):
        return jnp.where((cell == slots[0, s]) & (s < live), s, table)

    inv_v[...] = lax.fori_loop(0, 192, find, jnp.full((8, 128), 192, jnp.int32), unroll=8)
    place_table = pltpu.make_async_copy(inv_v, inv, tsem.at[4])
    place_table.start()
    local[0].wait()
    pl.semaphore_wait(barrier, 17)

    def feature(i, lower=None):
        block = xpan.at[row_from(i)]
        return block if lower is None else block.at[pl.ds(128 * lower, 128)]

    def pass_on(i, lower, name, to):
        send(feature(i, lower), feature(i, lower), "feat", name, at_row(to))

    pass_on(0, 1, 0, 4)
    for i in (1, 3, 2):
        pass_on(0, None, i, i)
    pass_on(0, 0, 4, 4)
    place_table.wait()
    local[1].wait()

    two = jnp.int32(2)

    def spot(zt):
        return zt, lax.div(zt, two), lax.rem(zt, two) * 64

    def pair(n, at):
        return jnp.concatenate([tiles[inv[n, at]], tiles[inv[n, at + 1]]], axis=1)

    def product(where, kt, blocks):
        _, half, begin = where
        begin = begin + kt * 32
        total = None
        for p in blocks:
            at = begin + 2 * p
            rows = [pair(half + (q // 2) * 4, at + (q % 2) * 16) for q in range(4)]
            part = jnp.dot(jnp.concatenate(rows, axis=0), xpan[p], preferred_element_type=F32)
            total = part if total is None else total + part
        return total

    @pl.loop(0, 16)
    def _(j):
        zt, kt = lax.div(j, two), lax.rem(j, two)
        pacc[zt, kt] = product(spot(zt), kt, [r])

    arrive(feature(4, 1), "feat", 0)
    for i in (1, 3, 2):
        pass_on(4, 1, 4 + i, i)
    for i in (1, 3):
        arrive(feature(i), "feat", i)
        pass_on(i, 0, 8 + i, 4)
    late = [row_from(i) for i in (4, 5, 7, 6)]

    def add_early(first, last, places):
        @pl.loop(first, last)
        def _(j):
            zt, kt = lax.div(j, two), lax.rem(j, two)
            pacc[zt, kt] += product(spot(zt), kt, [row_from(i) for i in places])

    add_early(0, 8, (1, 3))
    arrive(feature(2), "feat", 2)
    pass_on(2, 0, 10, 4)
    add_early(8, 16, (1, 3))
    add_early(0, 16, (2,))
    arrive(feature(4, 0), "feat", 4)
    for i in (1, 3, 2):
        arrive(feature(4 + i, 1), "feat", 4 + i)
        arrive(feature(4 + i, 0), "feat", 8 + i)

    def side(q):
        return xl if q else ox

    def forward(g, h):
        zt = (z + DIST[g] + 8) % 8
        kt = k if h else ok
        pacc[zt, kt] += product(spot(zt), kt, late)
        if h == 0:
            for q in range(2):
                ks[g, q] = pacc[zt, kt, pl.ds(q * N, N)].astype(BF16)
            send(ks.at[g], kr.at[g], "core", g, at_core())

    def chip_sum(g, q, first, last):
        zt, x = (z + DIST[g] + 8) % 8, side(q)
        return pacc[zt, k, pl.ds(x * N + first, last - first)] + kr[g, x, first:last].astype(F32)

    def way(d):
        return (0, 4 - d) if d > 0 else (1, 4 + d)

    def chip(g):
        arrive(kr.at[g], "core", g)
        sxs[g] = chip_sum(g, 0, 0, A).astype(BF16)
        send(sxs.at[g], rx.at[g], "xrow", g, at_x())
        sx[g] = chip_sum(g, 1, 0, A)

    def ring_z(g, q):
        s = chip_sum(g, q, A, N)
        w, step = (q, 0) if DIST[g] == 4 else way(DIST[g])
        if step > 1 or (step == 1 and q == w):
            arrive(rz.at[w, step - 1, q], "ringz", (w * 4 + step - 1) * 2 + q)
            s = s + rz[w, step - 1, q].astype(F32)
        zs[g, q] = s.astype(BF16)
        send(zs.at[g, q], rz.at[w, step, q], "ringz", (w * 4 + step) * 2 + q, at_z(1 - 2 * w))

    def ring_x(g):
        d = DIST[g]
        arrive(rx.at[g], "xrow", g)
        s = sx[g] + rx[g].astype(F32)
        if d == 4:
            qs[g] = s.astype(BF16)
            for w in range(2):
                rows = pl.ds(w * (A // 2), A // 2)
                send(qs.at[g, rows], rq.at[w, 0, rows], "ringx", w * 4, at_z(1 - 2 * w))
            return
        w, step = way(d)
        if step == 1:
            rows = pl.ds(w * (A // 2), A // 2)
            arrive(rq.at[w, 0, rows], "ringx", w * 4)
            sx[g] = s
            sx[g, rows] += rq[w, 0, rows].astype(F32)
            s = sx[g]
        else:
            arrive(rq.at[w, step - 1], "ringx", w * 4 + step - 1)
            s = s + rq[w, step - 1].astype(F32)
        qs[g] = s.astype(BF16)
        send(qs.at[g], rq.at[w, step], "ringx", w * 4 + step, at_z(1 - 2 * w))

    def last_z(q):
        for w in range(2):
            arrive(rz.at[w, 3, q], "ringz", (w * 4 + 3) * 2 + q)
        s = chip_sum(7, q, A, N) + rz[0, 3, q].astype(F32) + rz[1, 3, q].astype(F32)
        if q == 0:
            xfs[...] = s.astype(BF16)
            send(xfs, xfr, "xfin", 0, at_x())
        else:
            zf[...] = s

    for op in SUMS:
        if op[:2] == "Fa":
            forward(int(op[2]), 0)
        elif op[:2] == "Fb":
            forward(int(op[2]), 1)
        elif op[0] == "S":
            chip(int(op[1]))
        elif op[0] == "Z":
            ring_z(int(op[1]), int(op[2]))
        elif op[0] == "X":
            ring_x(int(op[1]))
        elif op in ("P0", "P1"):
            last_z(int(op[1]))
    arrive(rx.at[7], "xrow", 7)
    for w in range(2):
        arrive(rq.at[w, 3], "ringx", w * 4 + 3)
    head = (sx[7] + rx[7].astype(F32) + rq[0, 3].astype(F32) + rq[1, 3].astype(F32)).astype(BF16)
    arrive(xfr, "xfin", 0)
    tail = (zf[...] + xfr[...].astype(F32)).astype(BF16)
    local[2].wait()
    local[3].wait()

    hidden = jnp.concatenate([head, tail], axis=0)
    preact = jnp.dot(hidden, weight[...], preferred_element_type=F32)
    sig = jax.nn.sigmoid(preact)
    layer_out[...] = (preact * sig).astype(BF16)
    act = (cot[...].astype(F32) * sig * (1.0 + preact * (1.0 - sig))).astype(BF16)
    hp[z, k, xl] = jnp.dot(weight[...], act.T, preferred_element_type=F32).astype(BF16)

    head_rows, tail_rows = pl.ds(0, B), pl.ds(B, N - B)
    mine = hp.at[z, k, xl]
    mine_head, mine_tail = mine.at[head_rows], mine.at[tail_rows]
    send(mine_tail, mine_tail, "xv", 0, at_x())
    send(mine_head, mine_head, "head", 0, at_z(1))
    send(mine_head, mine_head, "head", 4, at_z(-1))
    send(mine_head, mine_head, "xu", 0, at_x())
    send(mine_tail, mine_tail, "tail", 0, at_z(1))
    send(mine_tail, mine_tail, "tail", 4, at_z(-1))

    def place(d):
        return (z + d + 8) % 8

    def came_from(w, step):
        return place(-1 - step) if w == 0 else place(1 + step)

    def number(d):
        return d if d >= 0 else 8 + d

    def head_step(w, step):
        dist = 4 if step == 3 else (1 + step if w else -1 - step)
        rows = hp.at[came_from(w, step), k, xl, head_rows]
        arrive(rows, "head", w * 4 + step)
        if step < 2 or (step == 2 and w == 0):
            send(rows, rows, "head", w * 4 + step + 1, at_z(1 - 2 * w))
        send(rows, rows, "xu", number(dist), at_x())

    def tail_step(w, step):
        rows = hp.at[came_from(w, step), k, xl, tail_rows]
        arrive(rows, "tail", w * 4 + step)
        if step < 2 or (step == 2 and w == 1):
            send(rows, rows, "tail", w * 4 + step + 1, at_z(1 - 2 * w))

    def part_step(w, step):
        to = at_z(1 - 2 * w)
        block = hp.at[came_from(w, step), k, ox]
        rows = block.at[tail_rows] if step < 3 else block.at[pl.ds(B + w * 64, 64)]
        arrive(rows, "part", w * 4 + step)
        if step < 2:
            send(rows, rows, "part", w * 4 + step + 1, to)
        elif step == 2:
            half = block.at[pl.ds(B + w * 64, 64)]
            send(half, half, "part", w * 4 + 3, to)

    def share(d):
        block = hp.at[place(d), k, ox, head_rows]
        arrive(block, "xu", number(d))
        both = hp.at[place(d), k]
        send(both, both, "pair", number(d), at_core())

    def have(d):
        arrive(hp.at[place(d), ok], "pair", number(d))

    def add_products(where, blocks, places, first=False):
        zt, half, begin = where
        left = jnp.concatenate([hp[zt, u, v] for u, v in blocks], axis=1)
        totals = []
        for n in places:
            rows = [
                pair(half + v * 4, begin + u * 32 + 2 * n + q * 16) for u, v in blocks for q in range(2)
            ]
            totals.append(jnp.dot(left, jnp.concatenate(rows, axis=0), preferred_element_type=F32))
        for n, total in zip(places, totals):
            if first:
                acc[n] = total
            else:
                acc[n] += total

    every = [(0, 0), (0, 1), (1, 0), (1, 1)]
    others = [(k, ox), (ok, xl), (ok, ox)]

    def own_block(d):
        where = spot(place(d))

        for n in (0, 4):
            add_products(where, [(k, xl)], [n, n + 1, n + 2, n + 3], d == 0)

    def backward(d, part):
        if part == 0:
            have(d)
        where = spot(place(d))
        add_products(where, others if abs(d) < 2 else every, [2 * part, 2 * part + 1])

    def x_tail():
        rows = hp.at[z, k, ox, tail_rows]
        arrive(rows, "xv", 0)
        send(rows, rows, "part", 0, at_z(1))
        send(rows, rows, "part", 4, at_z(-1))

    def gradient_step(step):
        if step == 1:
            w1s[...] = jnp.dot(hidden.T, act, preferred_element_type=F32).reshape(8, 32, N)
            for i in range(1, 8):
                send(w1s.at[row_of(i)], w1r.at[r], "w1", i, at_row(i))
        elif step == 2:
            for i in range(1, 8):
                arrive(w1r.at[row_from(i)], "w1", i)
            w1r[r] = w1s[r]
            s = w1r[0]
            for i in range(1, 8):
                s = s + w1r[i]
            for i in range(8):
                w2s[i] = s[(i // 2) * 8:(i // 2) * 8 + 8, (i % 2) * 128:(i % 2) * 128 + 128]
            for i in range(1, 8):
                send(w2s.at[place(i)], w2r.at[z], "w2", i, at_z(i))
        elif step == 3:
            for i in range(1, 8):
                arrive(w2r.at[place(-i)], "w2", i)
            w2r[z] = w2s[z]
            s = w2r[0]
            for i in range(1, 8):
                s = s + w2r[i]
            w3r[xl * 2 + k] = s
            for i in range(1, 4):
                send(w3r.at[xl * 2 + k], w3r.at[xl * 2 + k], "w3", i, at_mate(i))
        elif step == 4:
            for i in range(1, 4):
                arrive(w3r.at[((xl + i // 2) % 2) * 2 + (k + i % 2) % 2], "w3", i)
            w4r[r] = (w3r[0] + w3r[1]) + (w3r[2] + w3r[3])
            for i in range(1, 8):
                send(w4r.at[r], w4r.at[r], "w4", i, at_row(i))
        else:
            for i in range(1, 8):
                arrive(w4r.at[row_from(i)], "w4", i)
            w5r[z] = w4r[...]
            for i in range(1, 8):
                send(w5r.at[z], w5r.at[z], "w5", i, at_z(i))

    for op in GATHER:
        if op[:2] == "OH":
            head_step(int(op[2]), int(op[3]))
        elif op[:2] == "OT":
            tail_step(int(op[2]), int(op[3]))
        elif op[:2] == "PT":
            part_step(int(op[2]), int(op[3]))
        elif op[:2] == "SH":
            share(int(op[2:]))
        elif op[0] == "B":
            own_block(int(op[1:]))
        elif op[0] == "C":
            d, part = op[1:].split(",")
            backward(int(d), int(part))
        elif op[0] == "W":
            gradient_step(int(op[1]))
        else:
            x_tail()

    have(3)
    have(4)
    far, farthest = spot(place(3)), spot(place(4))

    for group in ((6, 5), (7, 2), (4, 1), (3, 0)):
        for where in (far, farthest):
            add_products(where, every, [row_of(i) for i in group])
        for i in group:
            if i:
                gs[row_of(i)] = acc[row_of(i)].astype(BF16)
                send(gs.at[row_of(i)], gr.at[r], "grad", i, at_row(i))

    gradient_step(5)
    s = acc[r]
    for i in (6, 5, 7, 2, 4, 1, 3):
        arrive(gr.at[row_from(i)], "grad", i)
        s = s + gr[row_from(i)].astype(F32)
    feature_grad[...] = s.astype(BF16).T
    for i in range(1, 8):
        arrive(w5r.at[place(-i)], "w5", i)
    for i in range(8):
        for j in range(8):
            first = j * 32 + (i // 2) * 8
            weight_grad[first:first + 8, (i % 2) * 128:(i % 2) * 128 + 128] = w5r[i, j] * (65536.0 ** -0.5)
    for d in sent:
        d.wait_send()


def hand_over(a, b, c, a_out, b_out, c_out):
    a_out[...] = a[...]
    b_out[...] = b[...]
    c_out[...] = c[...]


def body(features, edge_tiles, tile_slot, tile_count, weight, cotangent):
    vmem = pl.BlockSpec(memory_space=pltpu.VMEM)

    def buf(*shape, dtype=BF16):
        return pltpu.VMEM(shape, dtype)

    hbm = pl.BlockSpec(memory_space=pl.ANY)
    smem = pl.BlockSpec(memory_space=pltpu.SMEM)
    shapes = (
        jax.ShapeDtypeStruct((N, N), BF16),
        jax.ShapeDtypeStruct((N, N), F32),
        jax.ShapeDtypeStruct((N, N), BF16),
    )
    results = pl.pallas_call(
        kernel,
        out_shape=shapes,
        in_specs=[smem, smem, hbm, hbm, hbm, hbm],
        out_specs=(vmem, vmem, vmem),
        scratch_shapes=[
            buf(193, 128, 128),
            buf(8, N, N),
            buf(8, 2, 2 * N, N, dtype=F32),
            buf(8, 2, N, N),
            buf(8, 2, N, N),
            buf(8, A, N),
            buf(8, A, N, dtype=F32),
            buf(8, A, N),
            buf(7, 2, N - A, N),
            buf(2, 4, 2, N - A, N),
            buf(7, A, N),
            buf(2, 4, A, N),
            buf(N - A, N),
            buf(N - A, N),
            buf(N - A, N, dtype=F32),
            buf(8, 2, 2, N, N),
            buf(8, N, N, dtype=F32),
            buf(8, 32, N, dtype=F32),
            buf(8, 32, N, dtype=F32),
            buf(8, 8, 128, dtype=F32),
            buf(8, 8, 128, dtype=F32),
            buf(4, 8, 128, dtype=F32),
            buf(8, 8, 128, dtype=F32),
            buf(8, 8, 8, 128, dtype=F32),
            buf(8, N, N),
            buf(8, N, N),
            buf(N, N),
            buf(N, N),
            buf(8, 128, dtype=jnp.int32),
            pltpu.SMEM((8, 128), jnp.int32),
            pltpu.SemaphoreType.DMA((TOTAL,)),
            pltpu.SemaphoreType.DMA((TOTAL,)),
            pltpu.SemaphoreType.DMA((5,)),
        ],
        compiler_params=pltpu.CompilerParams(
            collective_id=0, has_side_effects=True, vmem_limit_bytes=56 * 2**20
        ),
    )(tile_slot, tile_count, features, edge_tiles.reshape(192, 128, 128), weight, cotangent)
    return pl.pallas_call(
        hand_over,
        out_shape=shapes,
        in_specs=[vmem] * 3,
        out_specs=(vmem,) * 3,
    )(*results)


def solution(mesh):
    in_specs = (
        P(("col", "row"), None),
        P("row", "col", None, None),
        P("row", "col"),
        P("row", "col"),
        P(),
        P(("row", "col"), None),
    )
    out_specs = (P(("row", "col"), None), P(), P(("col", "row"), None))
    return jax.shard_map(body, mesh=mesh, in_specs=in_specs, out_specs=out_specs, check_vma=False)
```

```python
import functools

import jax
import jax.numpy as jnp
from jax import lax
from jax.experimental import pallas as pl
from jax.experimental.pallas import tpu as pltpu
from jax.sharding import PartitionSpec as P

F32 = jnp.float32
BF16 = jnp.bfloat16
MESH = pl.DeviceIdType.MESH
N = 256
A = 128
B = 128
DIST = (4, 3, -3, 2, -2, 1, -1, 0)
SEMS = dict(
    feat=12, core=8, xrow=8, ringz=16, ringx=8, xfin=1,
    head=8, tail=8, part=8, xv=1, xu=8, pair=8,
    w1=8, w2=8, w3=4, w4=8, w5=8, grad=8,
)
SUMS = (
    "Fa0", "Fb0", "Fa1", "Fb1", "S0", "Z00", "Z01", "Fa2", "S1", "Z11", "Fb2", "Fa3", "S2", "Z20", "Fb3", "X0", "Z10",
    "Z21", "S3", "Fa4", "Fb4", "Z31", "Fa5", "S4", "Z40", "X1", "Fb5", "X2", "S5", "Z30", "Fa6", "Z41", "Fb6", "Z51",
    "Fa7", "S6", "Z60", "X3", "Fb7", "X4", "S7", "Z50", "Z61", "X5", "X6", "P0", "P1", "P2", "P3",
)
GATHER = (
    "B0", "OH00", "OH10", "V", "W1", "OT10", "OT00", "SH0", "B1", "B-1", "C0,0", "C0,1", "OH01", "OH11", "C0,2",
    "C0,3", "PT00", "SH-1", "PT10", "SH1", "OT01", "OT11", "C-1,0", "C-1,1", "W2", "C-1,2", "C-1,3", "OH12", "OH02",
    "C1,0", "C1,1", "PT01", "PT11", "SH-2", "C1,2", "C1,3", "SH2", "OT02", "OT12", "C-2,0", "C-2,1", "OH03", "C-2,2",
    "C-2,3", "C2,0", "PT02", "SH-3", "PT12", "SH3", "C2,1", "W3", "C2,2", "OT13", "C2,3", "C-3,0", "C-3,1", "W4", "C-3,2",
    "PT13", "PT03", "SH4", "C-3,3",
)
OFFSET = {}
TOTAL = 0
for _name, _count in SEMS.items():
    OFFSET[_name] = TOTAL
    TOTAL += _count


def kernel(
    slots, count, feat, tiles_hbm, weight_hbm, cot_hbm,
    layer_out, weight_grad, feature_grad,
    tiles, xpan, pacc, ks, kr, sxs, sx, rx, zs, rz, qs, rq, xfs, xfr, zf,
    hp, acc, w1s, w1r, w2s, w2r, w3r, w4r, w5r, gs, gr, weight, cot, inv_v, inv,
    ssem, rsem, tsem,
):
    r = lax.axis_index("row")
    c = lax.axis_index("col")
    xh, y = r // 4, r % 4
    xl, z, k = c // 16, (c % 16) // 2, c % 2
    ox, ok = 1 - xl, 1 - k

    def row_of(i):
        return ((xh + i // 4) % 2) * 4 + (y + i % 4) % 4

    def row_from(i):
        return ((xh + i // 4) % 2) * 4 + (y + 4 - i % 4) % 4

    def at_row(i):
        return (row_of(i), c)

    def at_z(d):
        return (r, xl * 16 + ((z + d + 8) % 8) * 2 + k)

    def at_x():
        return (r, ox * 16 + z * 2 + k)

    def at_core():
        return (r, xl * 16 + z * 2 + ok)

    def at_mate(i):
        return (r, ((xl + i // 2) % 2) * 16 + z * 2 + (k + i % 2) % 2)

    sent = []

    def desc(src, dst, name, i, to):
        return pltpu.make_async_remote_copy(
            src_ref=src, dst_ref=dst, send_sem=ssem.at[OFFSET[name] + i],
            recv_sem=rsem.at[OFFSET[name] + i], device_id=to, device_id_type=MESH,
        )

    def send(src, dst, name, i, to):
        d = desc(src, dst, name, i, to)
        d.start()
        sent.append(d)

    def arrive(dst, name, i):
        desc(dst, dst, name, i, at_core()).wait_recv()

    barrier = pltpu.get_barrier_semaphore()
    for i in range(1, 8):
        pl.semaphore_signal(barrier, inc=1, device_id=at_row(i), device_id_type=MESH)
        pl.semaphore_signal(barrier, inc=1, device_id=at_z(i), device_id_type=MESH)
    for i in range(1, 4):
        pl.semaphore_signal(barrier, inc=1, device_id=at_mate(i), device_id_type=MESH)
    local = [
        pltpu.make_async_copy(src, dst, tsem.at[i])
        for i, (src, dst) in enumerate((
            (feat, xpan.at[r]), (tiles_hbm, tiles.at[pl.ds(0, 192)]), (weight_hbm, weight), (cot_hbm, cot),
        ))
    ]
    for copy in local:
        copy.start()
    tiles[192] = jnp.zeros((128, 128), BF16)
    cell = lax.broadcasted_iota(jnp.int32, (8, 128), 0) * 128 + lax.broadcasted_iota(jnp.int32, (8, 128), 1)
    live = count[0, 0]

    def find(s, table):
        return jnp.where((cell == slots[0, s]) & (s < live), s, table)

    inv_v[...] = lax.fori_loop(0, 192, find, jnp.full((8, 128), 192, jnp.int32), unroll=8)
    place_table = pltpu.make_async_copy(inv_v, inv, tsem.at[4])
    place_table.start()
    local[0].wait()
    pl.semaphore_wait(barrier, 17)

    def feature(i, lower=None):
        block = xpan.at[row_from(i)]
        return block if lower is None else block.at[pl.ds(128 * lower, 128)]

    def pass_on(i, lower, name, to):
        send(feature(i, lower), feature(i, lower), "feat", name, at_row(to))

    pass_on(0, 1, 0, 4)
    for i in (1, 3, 2):
        pass_on(0, None, i, i)
    pass_on(0, 0, 4, 4)
    place_table.wait()
    local[1].wait()

    two = jnp.int32(2)

    def spot(zt):
        return zt, lax.div(zt, two), lax.rem(zt, two) * 64

    def pair(n, at):
        return jnp.concatenate([tiles[inv[n, at]], tiles[inv[n, at + 1]]], axis=1)

    def product(where, kt, blocks):
        _, half, begin = where
        begin = begin + kt * 32
        total = None
        for p in blocks:
            at = begin + 2 * p
            rows = [pair(half + (q // 2) * 4, at + (q % 2) * 16) for q in range(4)]
            part = jnp.dot(jnp.concatenate(rows, axis=0), xpan[p], preferred_element_type=F32)
            total = part if total is None else total + part
        return total

    @pl.loop(0, 16)
    def _(j):
        zt, kt = lax.div(j, two), lax.rem(j, two)
        pacc[zt, kt] = product(spot(zt), kt, [r])

    arrive(feature(4, 1), "feat", 0)
    for i in (1, 3, 2):
        pass_on(4, 1, 4 + i, i)
    for i in (1, 3):
        arrive(feature(i), "feat", i)
        pass_on(i, 0, 8 + i, 4)
    late = [row_from(i) for i in (4, 5, 7, 6)]

    def add_early(first, last, places):
        @pl.loop(first, last)
        def _(j):
            zt, kt = lax.div(j, two), lax.rem(j, two)
            pacc[zt, kt] += product(spot(zt), kt, [row_from(i) for i in places])

    add_early(0, 8, (1, 3))
    arrive(feature(2), "feat", 2)
    pass_on(2, 0, 10, 4)
    add_early(8, 16, (1, 3))
    add_early(0, 16, (2,))
    arrive(feature(4, 0), "feat", 4)
    for i in (1, 3, 2):
        arrive(feature(4 + i, 1), "feat", 4 + i)
        arrive(feature(4 + i, 0), "feat", 8 + i)

    def side(q):
        return xl if q else ox

    def forward(g, h):
        zt = (z + DIST[g] + 8) % 8
        kt = k if h else ok
        pacc[zt, kt] += product(spot(zt), kt, late)
        if h == 0:
            for q in range(2):
                ks[g, q] = pacc[zt, kt, pl.ds(q * N, N)].astype(BF16)
            send(ks.at[g], kr.at[g], "core", g, at_core())

    def chip_sum(g, q, first, last):
        zt, x = (z + DIST[g] + 8) % 8, side(q)
        return pacc[zt, k, pl.ds(x * N + first, last - first)] + kr[g, x, first:last].astype(F32)

    def way(d):
        return (0, 4 - d) if d > 0 else (1, 4 + d)

    def chip(g):
        arrive(kr.at[g], "core", g)
        sxs[g] = chip_sum(g, 0, 0, A).astype(BF16)
        send(sxs.at[g], rx.at[g], "xrow", g, at_x())
        sx[g] = chip_sum(g, 1, 0, A)

    def ring_z(g, q):
        s = chip_sum(g, q, A, N)
        w, step = (q, 0) if DIST[g] == 4 else way(DIST[g])
        if step > 1 or (step == 1 and q == w):
            arrive(rz.at[w, step - 1, q], "ringz", (w * 4 + step - 1) * 2 + q)
            s = s + rz[w, step - 1, q].astype(F32)
        zs[g, q] = s.astype(BF16)
        send(zs.at[g, q], rz.at[w, step, q], "ringz", (w * 4 + step) * 2 + q, at_z(1 - 2 * w))

    def ring_x(g):
        d = DIST[g]
        arrive(rx.at[g], "xrow", g)
        s = sx[g] + rx[g].astype(F32)
        if d == 4:
            qs[g] = s.astype(BF16)
            for w in range(2):
                rows = pl.ds(w * (A // 2), A // 2)
                send(qs.at[g, rows], rq.at[w, 0, rows], "ringx", w * 4, at_z(1 - 2 * w))
            return
        w, step = way(d)
        if step == 1:
            rows = pl.ds(w * (A // 2), A // 2)
            arrive(rq.at[w, 0, rows], "ringx", w * 4)
            sx[g] = s
            sx[g, rows] += rq[w, 0, rows].astype(F32)
            s = sx[g]
        else:
            arrive(rq.at[w, step - 1], "ringx", w * 4 + step - 1)
            s = s + rq[w, step - 1].astype(F32)
        qs[g] = s.astype(BF16)
        send(qs.at[g], rq.at[w, step], "ringx", w * 4 + step, at_z(1 - 2 * w))

    def last_z(q):
        for w in range(2):
            arrive(rz.at[w, 3, q], "ringz", (w * 4 + 3) * 2 + q)
        s = chip_sum(7, q, A, N) + rz[0, 3, q].astype(F32) + rz[1, 3, q].astype(F32)
        if q == 0:
            xfs[...] = s.astype(BF16)
            send(xfs, xfr, "xfin", 0, at_x())
        else:
            zf[...] = s

    for op in SUMS:
        if op[:2] == "Fa":
            forward(int(op[2]), 0)
        elif op[:2] == "Fb":
            forward(int(op[2]), 1)
        elif op[0] == "S":
            chip(int(op[1]))
        elif op[0] == "Z":
            ring_z(int(op[1]), int(op[2]))
        elif op[0] == "X":
            ring_x(int(op[1]))
        elif op in ("P0", "P1"):
            last_z(int(op[1]))
    arrive(rx.at[7], "xrow", 7)
    for w in range(2):
        arrive(rq.at[w, 3], "ringx", w * 4 + 3)
    head = (sx[7] + rx[7].astype(F32) + rq[0, 3].astype(F32) + rq[1, 3].astype(F32)).astype(BF16)
    arrive(xfr, "xfin", 0)
    tail = (zf[...] + xfr[...].astype(F32)).astype(BF16)
    local[2].wait()
    local[3].wait()

    hidden = jnp.concatenate([head, tail], axis=0)
    preact = jnp.dot(hidden, weight[...], preferred_element_type=F32)
    sig = jax.nn.sigmoid(preact)
    layer_out[...] = (preact * sig).astype(BF16)
    act = (cot[...].astype(F32) * sig * (1.0 + preact * (1.0 - sig))).astype(BF16)
    hp[z, k, xl] = jnp.dot(weight[...], act.T, preferred_element_type=F32).astype(BF16)

    head_rows, tail_rows = pl.ds(0, B), pl.ds(B, N - B)
    mine = hp.at[z, k, xl]
    mine_head, mine_tail = mine.at[head_rows], mine.at[tail_rows]
    send(mine_tail, mine_tail, "xv", 0, at_x())
    send(mine_head, mine_head, "head", 0, at_z(1))
    send(mine_head, mine_head, "head", 4, at_z(-1))
    send(mine_head, mine_head, "xu", 0, at_x())
    send(mine_tail, mine_tail, "tail", 0, at_z(1))
    send(mine_tail, mine_tail, "tail", 4, at_z(-1))

    def place(d):
        return (z + d + 8) % 8

    def came_from(w, step):
        return place(-1 - step) if w == 0 else place(1 + step)

    def number(d):
        return d if d >= 0 else 8 + d

    def head_step(w, step):
        dist = 4 if step == 3 else (1 + step if w else -1 - step)
        rows = hp.at[came_from(w, step), k, xl, head_rows]
        arrive(rows, "head", w * 4 + step)
        if step < 2 or (step == 2 and w == 0):
            send(rows, rows, "head", w * 4 + step + 1, at_z(1 - 2 * w))
        send(rows, rows, "xu", number(dist), at_x())

    def tail_step(w, step):
        rows = hp.at[came_from(w, step), k, xl, tail_rows]
        arrive(rows, "tail", w * 4 + step)
        if step < 2 or (step == 2 and w == 1):
            send(rows, rows, "tail", w * 4 + step + 1, at_z(1 - 2 * w))

    def part_step(w, step):
        to = at_z(1 - 2 * w)
        block = hp.at[came_from(w, step), k, ox]
        rows = block.at[tail_rows] if step < 3 else block.at[pl.ds(B + w * 64, 64)]
        arrive(rows, "part", w * 4 + step)
        if step < 2:
            send(rows, rows, "part", w * 4 + step + 1, to)
        elif step == 2:
            half = block.at[pl.ds(B + w * 64, 64)]
            send(half, half, "part", w * 4 + 3, to)

    def share(d):
        block = hp.at[place(d), k, ox, head_rows]
        arrive(block, "xu", number(d))
        both = hp.at[place(d), k]
        send(both, both, "pair", number(d), at_core())

    def have(d):
        arrive(hp.at[place(d), ok], "pair", number(d))

    def add_products(where, blocks, places, first=False):
        zt, half, begin = where
        left = jnp.concatenate([hp[zt, u, v] for u, v in blocks], axis=1)
        totals = []
        for n in places:
            rows = [
                pair(half + v * 4, begin + u * 32 + 2 * n + q * 16) for u, v in blocks for q in range(2)
            ]
            totals.append(jnp.dot(left, jnp.concatenate(rows, axis=0), preferred_element_type=F32))
        for n, total in zip(places, totals):
            if first:
                acc[n] = total
            else:
                acc[n] += total

    every = [(0, 0), (0, 1), (1, 0), (1, 1)]
    others = [(k, ox), (ok, xl), (ok, ox)]

    def own_block(d):
        where = spot(place(d))

        for n in (0, 4):
            add_products(where, [(k, xl)], [n, n + 1, n + 2, n + 3], d == 0)

    def backward(d, part):
        if part == 0:
            have(d)
        where = spot(place(d))
        add_products(where, others if abs(d) < 2 else every, [2 * part, 2 * part + 1])

    def x_tail():
        rows = hp.at[z, k, ox, tail_rows]
        arrive(rows, "xv", 0)
        send(rows, rows, "part", 0, at_z(1))
        send(rows, rows, "part", 4, at_z(-1))

    def gradient_step(step):
        if step == 1:
            w1s[...] = jnp.dot(hidden.T, act, preferred_element_type=F32).reshape(8, 32, N)
            for i in range(1, 8):
                send(w1s.at[row_of(i)], w1r.at[r], "w1", i, at_row(i))
        elif step == 2:
            for i in range(1, 8):
                arrive(w1r.at[row_from(i)], "w1", i)
            w1r[r] = w1s[r]
            s = w1r[0]
            for i in range(1, 8):
                s = s + w1r[i]
            for i in range(8):
                w2s[i] = s[(i // 2) * 8:(i // 2) * 8 + 8, (i % 2) * 128:(i % 2) * 128 + 128]
            for i in range(1, 8):
                send(w2s.at[place(i)], w2r.at[z], "w2", i, at_z(i))
        elif step == 3:
            for i in range(1, 8):
                arrive(w2r.at[place(-i)], "w2", i)
            w2r[z] = w2s[z]
            s = w2r[0]
            for i in range(1, 8):
                s = s + w2r[i]
            w3r[xl * 2 + k] = s
            for i in range(1, 4):
                send(w3r.at[xl * 2 + k], w3r.at[xl * 2 + k], "w3", i, at_mate(i))
        elif step == 4:
            for i in range(1, 4):
                arrive(w3r.at[((xl + i // 2) % 2) * 2 + (k + i % 2) % 2], "w3", i)
            w4r[r] = (w3r[0] + w3r[1]) + (w3r[2] + w3r[3])
            for i in range(1, 8):
                send(w4r.at[r], w4r.at[r], "w4", i, at_row(i))
        else:
            for i in range(1, 8):
                arrive(w4r.at[row_from(i)], "w4", i)
            w5r[z] = w4r[...]
            for i in range(1, 8):
                send(w5r.at[z], w5r.at[z], "w5", i, at_z(i))

    for op in GATHER:
        if op[:2] == "OH":
            head_step(int(op[2]), int(op[3]))
        elif op[:2] == "OT":
            tail_step(int(op[2]), int(op[3]))
        elif op[:2] == "PT":
            part_step(int(op[2]), int(op[3]))
        elif op[:2] == "SH":
            share(int(op[2:]))
        elif op[0] == "B":
            own_block(int(op[1:]))
        elif op[0] == "C":
            d, part = op[1:].split(",")
            backward(int(d), int(part))
        elif op[0] == "W":
            gradient_step(int(op[1]))
        else:
            x_tail()

    have(3)
    have(4)
    far, farthest = spot(place(3)), spot(place(4))

    for group in ((6, 5), (7, 2), (4, 1), (3, 0)):
        for where in (far, farthest):
            add_products(where, every, [row_of(i) for i in group])
        for i in group:
            if i:
                gs[row_of(i)] = acc[row_of(i)].astype(BF16)
                send(gs.at[row_of(i)], gr.at[r], "grad", i, at_row(i))

    gradient_step(5)
    s = acc[r]
    for i in (6, 5, 7, 2, 4, 1, 3):
        arrive(gr.at[row_from(i)], "grad", i)
        s = s + gr[row_from(i)].astype(F32)
    feature_grad[...] = s.astype(BF16).T
    for i in range(1, 8):
        arrive(w5r.at[place(-i)], "w5", i)
    for i in range(8):
        for j in range(8):
            first = j * 32 + (i // 2) * 8
            weight_grad[first:first + 8, (i % 2) * 128:(i % 2) * 128 + 128] = w5r[i, j] * (65536.0 ** -0.5)
    for d in sent:
        d.wait_send()


def hand_over(a, b, c, a_out, b_out, c_out):
    a_out[...] = a[...]
    b_out[...] = b[...]
    c_out[...] = c[...]


def body(features, edge_tiles, tile_slot, tile_count, weight, cotangent):
    vmem = pl.BlockSpec(memory_space=pltpu.VMEM)

    def buf(*shape, dtype=BF16):
        return pltpu.VMEM(shape, dtype)

    hbm = pl.BlockSpec(memory_space=pl.ANY)
    smem = pl.BlockSpec(memory_space=pltpu.SMEM)
    shapes = (
        jax.ShapeDtypeStruct((N, N), BF16),
        jax.ShapeDtypeStruct((N, N), F32),
        jax.ShapeDtypeStruct((N, N), BF16),
    )
    results = pl.pallas_call(
        kernel,
        out_shape=shapes,
        in_specs=[smem, smem, hbm, hbm, hbm, hbm],
        out_specs=(vmem, vmem, vmem),
        scratch_shapes=[
            buf(193, 128, 128),
            buf(8, N, N),
            buf(8, 2, 2 * N, N, dtype=F32),
            buf(8, 2, N, N),
            buf(8, 2, N, N),
            buf(8, A, N),
            buf(8, A, N, dtype=F32),
            buf(8, A, N),
            buf(7, 2, N - A, N),
            buf(2, 4, 2, N - A, N),
            buf(7, A, N),
            buf(2, 4, A, N),
            buf(N - A, N),
            buf(N - A, N),
            buf(N - A, N, dtype=F32),
            buf(8, 2, 2, N, N),
            buf(8, N, N, dtype=F32),
            buf(8, 32, N, dtype=F32),
            buf(8, 32, N, dtype=F32),
            buf(8, 8, 128, dtype=F32),
            buf(8, 8, 128, dtype=F32),
            buf(4, 8, 128, dtype=F32),
            buf(8, 8, 128, dtype=F32),
            buf(8, 8, 8, 128, dtype=F32),
            buf(8, N, N),
            buf(8, N, N),
            buf(N, N),
            buf(N, N),
            buf(8, 128, dtype=jnp.int32),
            pltpu.SMEM((8, 128), jnp.int32),
            pltpu.SemaphoreType.DMA((TOTAL,)),
            pltpu.SemaphoreType.DMA((TOTAL,)),
            pltpu.SemaphoreType.DMA((5,)),
        ],
        compiler_params=pltpu.CompilerParams(
            collective_id=0, has_side_effects=True, vmem_limit_bytes=56 * 2**20
        ),
    )(tile_slot, tile_count, features, edge_tiles.reshape(192, 128, 128), weight, cotangent)
    return pl.pallas_call(
        hand_over,
        out_shape=shapes,
        in_specs=[vmem] * 3,
        out_specs=(vmem,) * 3,
    )(*results)


def solution(mesh):
    in_specs = (
        P(("col", "row"), None),
        P("row", "col", None, None),
        P("row", "col"),
        P("row", "col"),
        P(),
        P(("row", "col"), None),
    )
    out_specs = (P(("row", "col"), None), P(), P(("col", "row"), None))
    return jax.shard_map(body, mesh=mesh, in_specs=in_specs, out_specs=out_specs, check_vma=False)
```
